256 devices in a mesh: gx: 8 (over x, z_lo), gy: 4 (over y), gz: 8 (over z_hi, core).
Axes of the slice: x: 4, y: 4, z: 8 (z_hi: 4, z_lo: 2; z = z_hi * 2 + z_lo), core: 2. Of those that a mesh axis runs over, the one named last changes fastest.
Arguments:
- states: float32 [19, 128, 64, 1024], P(None, 'gx', 'gy', 'gz'), may hold values from 0 to 1
- active: int32 [16, 4, 8], P('gx', 'gy', 'gz'), may hold values 0 or 1
- fibre_index: int32 [16, 4, 8], P('gx', 'gy', 'gz'), may hold values from 0 to 63
- fibre_angle: float32 [2, 64], replicated, may hold values from -3.140625 to 3.140625
- conduct: float32 [2, 64], replicated, may hold values from 0.05 to 0.3
- gate_half: float32 [17], replicated, may hold values from 0.1 to 0.9
- gate_slope: float32 [17], replicated, may hold values from 0.05 to 0.3
- gate_tau: float32 [17], replicated, may hold values from 2 to 60
- conductance: float32 [17], replicated, may hold values from 0.005 to 0.05
- reversal: float32 [17], replicated, may hold values from -1 to 1.5
- block_elem: int32 [64, 32, 32], P('gx', 'gy', 'gz'), may hold values from 0 to 65535, as said below
- block_weight: float32 [64, 32, 32], P('gx', 'gy', 'gz'), may hold values from 0.5 to 1.5
- node_disp: float32 [3, 131072], P(None, ('gx', 'gy', 'gz')), may hold values from -0.15 to 0.15
- elem_node: int32 [8, 65536], P(None, ('gx', 'gy', 'gz')), may hold values from 0 to 404, as said below
- elem_fibre: int32 [65536], P(('gx', 'gy', 'gz')), may hold values from 0 to 63
- material: float32 [3], replicated, may hold values from 0.5 to 2
Outputs:
- new_states: float32 [19, 128, 64, 1024], P(None, 'gx', 'gy', 'gz')
- fine_disp: float32 [3, 128, 64, 1024], P(None, 'gx', 'gy', 'gz')
- node_residual: float32 [3, 131072], P(None, ('gx', 'gy', 'gz'))
The draws below stay inside these ranges and needn't reach their ends.
Inputs may be any that keep to these rules, and one draw needn't show every extreme that they name: `block_elem`: element numbers of the coarse partition: owner device e // 256, local element e % 256. Every element holds exactly one coupling block. Of the coupling blocks of one device at most 2 lie in elements of one owner device, and for every device some owner receives exactly 2 of them. `elem_node`: each column names eight distinct owner-local nodes of a hexahedral element of a structured partition, corner 4 i + 2 j + k at offset (i, j, k); neighbouring elements of one owner share nodes.
All inputs are finite; a program needn't handle non-finite values. No bound on the sum of `active` on one device may be relied on, other than what follows from the above.
Results may differ from the reference program's by a relative error of at most 0.0003.
Values sent between devices are 32-bit elements; how exact they have to be, the bound alone decides.
No kernel may reach another device: no remote copies, remote signals or barrier semaphores. Data moves between devices by JAX's collectives and lax.ppermute only.
A program may use at most 64 MiB of HBM per device.

```python
import math
import jax
import jax.numpy as jnp
from jax import lax

NSTATE = 19
NCH = 17
NF = 64
TLX = 8
TLY = 16
TLZ = 128
SBX = 2
SBY = 2
SBZ = 32
FINE_STEPS = 2
ELX = 8
ELY = 8
CX = 16
CY = 16
CZ = 128
NX = 128
NY = 64
NZ = 1024
TX = 16
TY = 4
TZ = 8
BX = 64
BY = 32
BZ = 32
ELZ = 4
ELEM_DEV = 256
NODE_DEV = 512
ELEMS = 65536
NODES = 131072


def draw_block_elem(key, part):
    grid_x = NX // CX
    grid_y = NY // CY
    grid_z = NZ // CZ
    device_count = grid_x * grid_y * grid_z
    blocks_x = CX // SBX
    blocks_y = CY // SBY
    blocks_z = CZ // SBZ
    block_count = blocks_x * blocks_y * blocks_z
    capacity = 2 * block_count // device_count
    halfcap = capacity // 2
    slot_count = device_count * capacity
    base = jax.random.fold_in(key, 7)
    first, second, third, fourth = jax.random.split(base, 4)
    shift_full = jax.random.randint(first, (), 0, device_count, dtype=jnp.int32)
    shift_empty = (shift_full + jax.random.randint(second, (), 1, device_count, dtype=jnp.int32)) % device_count
    sigma = jax.random.permutation(third, device_count).astype(jnp.int32)
    distance = (sigma[None, :] - sigma[:, None]) % device_count
    counts = halfcap + halfcap * (distance == shift_full).astype(jnp.int32) - halfcap * (distance == shift_empty).astype(jnp.int32)
    starts = jnp.cumsum(counts, axis=0) - counts

    def owner_perm(index):
        return jax.random.permutation(jax.random.fold_in(fourth, index), ELEM_DEV).astype(jnp.int32)
    perms = jax.vmap(owner_perm)(jnp.arange(device_count, dtype=jnp.int32))

    def one_device(index):
        inner = jax.random.fold_in(jax.random.fold_in(key, 13), index)
        owners = jnp.arange(device_count, dtype=jnp.int32)[:, None]
        ranks = jnp.arange(capacity, dtype=jnp.int32)[None, :]
        valid = ranks < counts[index][:, None]
        where = jnp.clip(starts[index][:, None] + ranks, 0, ELEM_DEV - 1)
        local = perms[owners, where]
        ids = (owners * ELEM_DEV + local).reshape(-1)
        places = jnp.arange(slot_count, dtype=jnp.int32)
        score = jnp.where(valid.reshape(-1), slot_count + places, places)
        unused, chosen = lax.top_k(score, block_count)
        order = jax.random.permutation(inner, block_count)
        return ids[chosen][order].reshape(blocks_x, blocks_y, blocks_z)
    every = jax.vmap(one_device)(jnp.arange(device_count, dtype=jnp.int32))
    every = every.reshape(grid_x, grid_y, grid_z, blocks_x, blocks_y, blocks_z)
    return every.transpose(0, 3, 1, 4, 2, 5).reshape(grid_x * blocks_x, grid_y * blocks_y, grid_z * blocks_z)


def draw_elem_node(key, part):
    device_count = ELEMS // ELEM_DEV
    used = (ELX + 1) * (ELY + 1) * (ELZ + 1)
    corner = jnp.arange(8, dtype=jnp.int32)[:, None]
    cell = jnp.arange(ELEM_DEV, dtype=jnp.int32)[None, :]
    node_x = cell // (ELY * ELZ) + corner // 4
    node_y = cell // ELZ % ELY + corner // 2 % 2
    node_z = cell % ELZ + corner % 2
    structured = (node_x * (ELY + 1) + node_y) * (ELZ + 1) + node_z

    def one_device(index):
        inner = jax.random.fold_in(jax.random.fold_in(key, 11), index)
        first, second = jax.random.split(inner)
        label = jax.random.permutation(first, used).astype(jnp.int32)
        order = jax.random.permutation(second, ELEM_DEV)
        return label[structured][:, order]
    every = jax.vmap(one_device)(jnp.arange(device_count, dtype=jnp.int32))
    return every.transpose(1, 0, 2).reshape(8, device_count * ELEM_DEV)


def place_ends(array, stream_key, low, top_value):
    longest = array.shape.index(max(array.shape))
    spots = []
    for shift in (0, 1):
        where = [jax.random.randint(jax.random.fold_in(stream_key, axis), (), 0, length) for axis, length in enumerate(array.shape)]
        where[longest] = (where[longest] + shift) % array.shape[longest]
        spots.append(tuple(where))
    return array.at[spots[0]].set(low).at[spots[1]].set(top_value)


def block_levels(stream_key, shape, cuts, low, largest):
    factor_of, own = 1.0, jax.random.fold_in(stream_key, 6)
    for dim, shards_of in cuts:
        draws = jnp.exp(jax.random.uniform(jax.random.fold_in(own, dim), (shards_of,), jnp.float32, low / len(cuts), largest / len(cuts)))
        factor_of = factor_of * jnp.repeat(draws, shape[dim] // shards_of).reshape([-1 if axis == dim else 1 for axis in range(len(shape))])
    return factor_of


def scatter_about(own_key, dims, deviation, bound, cuts=(), held_as=jnp.bfloat16):
    level = block_levels(own_key, dims, cuts, -0.22, 0.18) if cuts else 1.0
    drawn = jax.random.normal(own_key, dims, jnp.float32) * deviation * level
    return jnp.minimum(jnp.maximum(drawn, -bound), bound).astype(held_as)


def setup_inputs(seed: int = 0) -> dict:
    arg_keys = jax.random.split(jax.random.key(seed), 17)
    states = jnp.clip(1.0 * jax.random.uniform(arg_keys[0], (NSTATE, NX, NY, NZ), jnp.float32) ** block_levels(arg_keys[0], (NSTATE, NX, NY, NZ), ((1, 8), (2, 4), (3, 8)), -0.2, 0.2), 0.0, 1.0)
    active = place_ends((jax.random.randint(arg_keys[1], (TX, TY, TZ), 0, 4) < 3).astype(jnp.int32), jax.random.fold_in(arg_keys[1], 1), 0, 1)
    fibre_index = place_ends(jax.random.randint(arg_keys[2], (TX, TY, TZ), 0, NF), jax.random.fold_in(arg_keys[2], 1), 0, NF - 1).astype(jnp.int32)
    fibre_angle = jnp.clip(jax.random.uniform(arg_keys[3], (2, NF), jnp.float32, -3.140625, 3.140625), -3.140625, 3.140625)
    conduct = jnp.clip(jnp.exp(jax.random.uniform(arg_keys[4], (2, NF), jnp.float32, math.log(0.05), math.log(0.3))), 0.05, 0.3)
    gate_half = jnp.clip(jax.random.uniform(arg_keys[5], (NCH,), jnp.float32, 0.1, 0.9), 0.1, 0.9)
    gate_slope = jnp.clip(jnp.exp(jax.random.uniform(arg_keys[6], (NCH,), jnp.float32, math.log(0.05), math.log(0.3))), 0.05, 0.3)
    gate_tau = jnp.clip(jnp.exp(jax.random.uniform(arg_keys[7], (NCH,), jnp.float32, math.log(2.0), math.log(60.0))), 2.0, 60.0)
    conductance = jnp.clip(jnp.exp(jax.random.uniform(arg_keys[8], (NCH,), jnp.float32, math.log(0.005), math.log(0.05))), 0.005, 0.05)
    reversal = jnp.clip(jax.random.uniform(arg_keys[9], (NCH,), jnp.float32, -1.0, 1.5), -1.0, 1.5)
    block_elem = draw_block_elem(jax.random.fold_in(arg_keys[16], 71), 0)
    block_weight = jnp.clip(0.5 + 1.0 * jax.random.uniform(arg_keys[11], (BX, BY, BZ), jnp.float32) ** block_levels(arg_keys[11], (BX, BY, BZ), ((0, 8), (1, 4), (2, 8)), -0.2, 0.2), 0.5, 1.5)
    node_disp = scatter_about(arg_keys[12], (3, NODES), 0.05, 0.15, ((1, 256),), jnp.float32)
    elem_node = draw_elem_node(jax.random.fold_in(arg_keys[16], 71), 0)
    elem_fibre = place_ends(jax.random.randint(arg_keys[14], (ELEMS,), 0, NF), jax.random.fold_in(arg_keys[14], 1), 0, NF - 1).astype(jnp.int32)
    material = jnp.clip(jnp.exp(jax.random.uniform(arg_keys[15], (3,), jnp.float32, math.log(0.5), math.log(2.0))), 0.5, 2.0)
    return {"states": states, "active": active, "fibre_index": fibre_index, "fibre_angle": fibre_angle, "conduct": conduct, "gate_half": gate_half, "gate_slope": gate_slope, "gate_tau": gate_tau, "conductance": conductance, "reversal": reversal, "block_elem": block_elem, "block_weight": block_weight, "node_disp": node_disp, "elem_node": elem_node, "elem_fibre": elem_fibre, "material": material}


calcium_keep = 0.9
tension_half = 0.09
highest = lax.Precision.HIGHEST


def fibre_frame(first_angle, second_angle):
    return jnp.stack([jnp.cos(first_angle) * jnp.cos(second_angle), jnp.sin(first_angle) * jnp.cos(second_angle), jnp.sin(second_angle)], 0)


def coefficients(frame, along, across, live_tile):
    spread = along - across
    return jnp.stack([across + spread * frame[0] * frame[0], across + spread * frame[1] * frame[1], across + spread * frame[2] * frame[2], spread * frame[0] * frame[1], spread * frame[0] * frame[2], spread * frame[1] * frame[2]], 0) * live_tile


def expand(tiles):
    return jnp.repeat(jnp.repeat(jnp.repeat(tiles, TLX, 1), TLY, 2), TLZ, 3)


def ionic(states, live, gate_half, gate_slope, gate_tau, conductance, reversal):
    volt = states[0]
    shape = (gate_half.shape[0],) + (1,) * (states.ndim - 1)
    steady = jax.nn.sigmoid((volt[None] - gate_half.reshape(shape)) / gate_slope.reshape(shape))
    keeping = jnp.exp(-1.0 / gate_tau).reshape(shape)
    old_gates = states[1:NSTATE - 1]
    gates = steady + (old_gates - steady) * keeping
    current = jnp.sum(conductance.reshape(shape) * gates * (volt[None] - reversal.reshape(shape)), axis=0)
    vstar = volt - current
    calcium = states[NSTATE - 1] * calcium_keep + (1.0 - calcium_keep) * jax.nn.sigmoid(8.0 * (volt - 0.5))
    alive = live > 0.5
    gates = jnp.where(alive[None], gates, old_gates)
    vstar = jnp.where(alive, vstar, volt)
    calcium = jnp.where(alive, calcium, states[NSTATE - 1])
    return gates, vstar, calcium


def fluxes(padded, coef):
    grad_x = (padded[2:, 1:-1, 1:-1] - padded[:-2, 1:-1, 1:-1]) * 0.5
    grad_y = (padded[1:-1, 2:, 1:-1] - padded[1:-1, :-2, 1:-1]) * 0.5
    grad_z = (padded[1:-1, 1:-1, 2:] - padded[1:-1, 1:-1, :-2]) * 0.5
    return jnp.stack([coef[0] * grad_x + coef[3] * grad_y + coef[4] * grad_z, coef[3] * grad_x + coef[1] * grad_y + coef[5] * grad_z, coef[4] * grad_x + coef[5] * grad_y + coef[2] * grad_z], 0)


def divergence(flux):
    return (flux[0, 2:, 1:-1, 1:-1] - flux[0, :-2, 1:-1, 1:-1]) * 0.5 + (flux[1, 1:-1, 2:, 1:-1] - flux[1, 1:-1, :-2, 1:-1]) * 0.5 + (flux[2, 1:-1, 1:-1, 2:] - flux[2, 1:-1, 1:-1, :-2]) * 0.5


def corner_bits():
    corner = jnp.arange(8, dtype=jnp.int32)
    return jnp.stack([corner // 4, (corner // 2) % 2, corner % 2], 1).astype(jnp.float32)


def shape_gradients():
    return (2.0 * corner_bits() - 1.0) * 0.25


def blend_weights():
    bits = corner_bits()
    place = jnp.arange(SBX * SBY * SBZ, dtype=jnp.int32)
    along_x = ((place // (SBY * SBZ)).astype(jnp.float32) + 0.5) / SBX
    along_y = (((place // SBZ) % SBY).astype(jnp.float32) + 0.5) / SBY
    along_z = ((place % SBZ).astype(jnp.float32) + 0.5) / SBZ
    local = jnp.stack([along_x, along_y, along_z], 0)
    factor = jnp.where(bits[:, :, None] > 0.5, local[None], 1.0 - local[None])
    return factor[:, 0] * factor[:, 1] * factor[:, 2]


def element_forces(corner_disp, frame, tension, material):
    grads = shape_gradients()
    deform = jnp.einsum('iae,aj->ije', corner_disp, grads, precision=highest) + jnp.eye(3, dtype=jnp.float32)[:, :, None]
    cof = jnp.stack([
        jnp.stack([deform[1, 1] * deform[2, 2] - deform[1, 2] * deform[2, 1], deform[1, 2] * deform[2, 0] - deform[1, 0] * deform[2, 2], deform[1, 0] * deform[2, 1] - deform[1, 1] * deform[2, 0]], 0),
        jnp.stack([deform[0, 2] * deform[2, 1] - deform[0, 1] * deform[2, 2], deform[0, 0] * deform[2, 2] - deform[0, 2] * deform[2, 0], deform[0, 1] * deform[2, 0] - deform[0, 0] * deform[2, 1]], 0),
        jnp.stack([deform[0, 1] * deform[1, 2] - deform[0, 2] * deform[1, 1], deform[0, 2] * deform[1, 0] - deform[0, 0] * deform[1, 2], deform[0, 0] * deform[1, 1] - deform[0, 1] * deform[1, 0]], 0)], 0)
    volume = deform[0, 0] * cof[0, 0] + deform[0, 1] * cof[0, 1] + deform[0, 2] * cof[0, 2]
    inverse_t = cof / volume
    stretch = jnp.sum(deform * frame[None], axis=1)
    stress = material[0] * (deform - inverse_t) + material[1] * jnp.log(volume) * inverse_t + material[2] * tension * stretch[:, None] * frame[None]
    return jnp.einsum('ije,aj->iae', stress, grads, precision=highest)


def reference(states, active, fibre_index, fibre_angle, conduct, gate_half, gate_slope, gate_tau, conductance, reversal, block_elem, block_weight, node_disp, elem_node, elem_fibre, material):
    frame = fibre_frame(fibre_angle[0][fibre_index], fibre_angle[1][fibre_index])
    live_tile = (active > 0).astype(jnp.float32)
    coef = expand(coefficients(frame, conduct[0][fibre_index], conduct[1][fibre_index], live_tile))
    live = expand(live_tile[None])[0]
    for step in range(FINE_STEPS):
        gates, vstar, calcium = ionic(states, live, gate_half, gate_slope, gate_tau, conductance, reversal)
        flux = fluxes(jnp.pad(vstar, 1), coef)
        lap = divergence(jnp.pad(flux, ((0, 0), (1, 1), (1, 1), (1, 1))))
        states = jnp.concatenate([(vstar + live * lap)[None], gates, calcium[None]], 0)
    calcium = states[NSTATE - 1]
    tension = calcium * calcium / (calcium * calcium + tension_half)
    block_mean = tension.reshape(BX, SBX, BY, SBY, BZ, SBZ).mean(axis=(1, 3, 5)).reshape(-1)
    block_value = block_weight.reshape(-1) * block_mean
    flat_ids = block_elem.reshape(-1)
    elem_tension = jax.ops.segment_sum(block_value, flat_ids, num_segments=ELEMS)
    owner = jnp.arange(ELEMS, dtype=jnp.int32) // ELEM_DEV
    global_nodes = owner[None, :] * NODE_DEV + elem_node
    corner_disp = node_disp[:, global_nodes]
    elem_frame = fibre_frame(fibre_angle[0][elem_fibre], fibre_angle[1][elem_fibre])
    force = element_forces(corner_disp, elem_frame, elem_tension, material)
    flat_nodes = global_nodes.reshape(-1)
    node_residual = jnp.stack([jax.ops.segment_sum(force[k].reshape(-1), flat_nodes, num_segments=NODES) for k in range(3)], 0)
    block_nodes = (flat_ids // ELEM_DEV)[None, :] * NODE_DEV + elem_node[:, flat_ids]
    block_disp = node_disp[:, block_nodes]
    fine = jnp.einsum('cab,ap->cbp', block_disp, blend_weights(), precision=highest)
    fine_disp = fine.reshape(3, BX, BY, BZ, SBX, SBY, SBZ).transpose(0, 1, 4, 2, 5, 3, 6).reshape(3, NX, NY, NZ)
    return states, fine_disp, node_residual
```

```python
import functools

import jax
import jax.numpy as jnp
import numpy as np
from jax import lax
from jax.experimental import pallas as pl
from jax.experimental.pallas import tpu as pltpu
from jax.sharding import PartitionSpec as P

NSTATE, NCH, NF = 19, 17, 64
CX, CY, CZ = 16, 16, 128
ELEMS, SLOTS, NODES = 256, 256, 512
ALL = ("gx", "gy", "gz")
HIGHEST = lax.Precision.HIGHEST
F32, BF16 = jnp.float32, jnp.bfloat16
NT = (((1,), (1,)), ((), ()))
TN = (((0,), (0,)), ((), ()))
CORNERS = [(q // 4, q // 2 % 2, q % 2) for q in range(8)]
HEAD = 2


def iota(shape, dim):
    return lax.broadcasted_iota(jnp.int32, shape, dim)


def neighbour(pos_ref, sizes, step):
    at = [pos_ref[d] + step[d] for d in range(3)]
    ok = (at[0] >= 0) & (at[0] < sizes[0])
    for d in (1, 2):
        ok = ok & (at[d] >= 0) & (at[d] < sizes[d])
    row = (at[0] * sizes[1] + at[1]) * sizes[2] + at[2]
    return jnp.where(ok, row, 0), ok


def put_row(msg, row, ok, edge):
    base = pl.ds(pl.multiple_of(row // 8 * 8, 8), 8)
    here = iota((8, 128), 0) == jnp.where(ok, row % 8, -1)
    msg[base, 128:256] = jnp.where(here, edge, msg[base, 128:256])


def take_row(got, row, ok, lanes):
    rows = got[pl.ds(pl.multiple_of(row // 8 * 8, 8), 8), lanes]
    here = iota((8, 128), 0) == jnp.where(ok, row % 8, -1)
    return jnp.sum(jnp.where(here, rows, 0.0), axis=0, keepdims=True)


def parts3(x):
    first = x.astype(BF16)
    rest = x - first.astype(F32)
    second = rest.astype(BF16)
    third = (rest - second.astype(F32)).astype(BF16)
    return first, second, third


def frame_of(angles):
    a, b = angles[0:1, :], angles[1:2, :]
    return jnp.cos(a) * jnp.cos(b), jnp.sin(a) * jnp.cos(b), jnp.sin(b)


def gate_constants(half_ref, slope_ref, tau_ref, cond_ref, rev_ref, const):
    for c in range(NCH):
        scale = 0.5 / jnp.full((8, 128), slope_ref[c], F32)
        keep = jnp.exp(-1.0 / jnp.full((8, 128), tau_ref[c], F32))
        cond = jnp.full((8, 128), cond_ref[c], F32)
        const[c] = scale
        const[NCH + c] = -half_ref[c] * scale
        const[2 * NCH + c] = keep
        const[3 * NCH + c] = 0.5 * (1.0 - keep)
        const[4 * NCH + c] = cond
        const[5 * NCH + c] = cond * rev_ref[c]


def twice(x):
    return jnp.concatenate([x, x], 0)


def ionic_plane(volt, source, target, x, alive, const):
    total = jnp.zeros_like(volt)
    moment = jnp.zeros_like(volt)
    for c in range(NCH):
        rise = jnp.tanh(volt * twice(const[c]) + twice(const[NCH + c]))
        old = source[1 + c, x]
        lift = twice(const[3 * NCH + c])
        gate = old * twice(const[2 * NCH + c]) + (lift * rise + lift)
        total += gate * twice(const[4 * NCH + c])
        moment += gate * twice(const[5 * NCH + c])
        target[1 + c, x] = jnp.where(alive, gate, old)
    vstar = volt - (volt * total - moment)
    old = source[NSTATE - 1, x]
    calcium = old * 0.9 + 0.1 * (0.5 * jnp.tanh(4.0 * (volt - 0.5)) + 0.5)
    calcium = jnp.where(alive, calcium, old)
    target[NSTATE - 1, x] = calcium
    return jnp.where(alive, vstar, volt), calcium


def send_faces(v, pos_ref, sizes, xlo, xhi, ylo, yhi, zlo, zhi, msg, lines):
    xlo[...] = v[0:2]
    xhi[...] = v[14:16]
    ylo[...] = v[:, 0:8, :]
    yhi[...] = v[:, 8:16, :]
    row, lane = iota((8, 128), 0), iota((8, 128), 1)
    pick = ((row < 4) & (lane == jnp.where(row < 2, row, row + 124))).astype(F32)
    flat = v[...].reshape(CX * CY, CZ)
    ends = lax.dot_general(pick, flat, NT, precision=HIGHEST, preferred_element_type=F32)
    zlo[...] = ends[0:2]
    zhi[...] = ends[2:4]
    lines[0:16] = v[0]
    lines[16:32] = v[15]
    for x in range(CX):
        lines[32 + x : 33 + x] = v[x, 0:1, :]
        lines[48 + x : 49 + x] = v[x, 15:16, :]
    lines[64:128] = jnp.zeros((64, 128), F32)
    marks = lax.dot_general(pick, lines[...], NT, precision=HIGHEST, preferred_element_type=F32)
    for dx in (-1, 1):
        for dy in (-1, 1):
            peer, ok = neighbour(pos_ref, sizes, (dx, dy, 0))
            edge = v[15 if dx > 0 else 0, (15 if dy > 0 else 0) : (16 if dy > 0 else 1), :]

            put_row(msg, peer, ok, edge)

    for step in ((-1, 0), (1, 0), (0, -1), (0, 1)):
        for dz in (-1, 1):
            peer, ok = neighbour(pos_ref, sizes, (*step, dz))
            edge = marks[3:4] if dz > 0 else marks[0:1]

            put_row(msg, peer, ok, edge)


def heads(pos_ref, sizes, got, step):
    row, ok = neighbour(pos_ref, sizes, step)
    return take_row(got, row, ok, slice(0, 128))


def entry(head, tile, which):
    lane = HEAD + 7 * tile + which
    return head[:, lane : lane + 1]


def edges_of(pos_ref, sizes, got, step):
    row, ok = neighbour(pos_ref, sizes, step)
    return take_row(got, row, ok, slice(128, 256))


def tile_planes(pos_ref, sizes, got1, cx, cy, cz):
    own = heads(pos_ref, sizes, got1, (0, 0, 0))
    ends = {s: heads(pos_ref, sizes, got1, s) for s in ((-1, 0, 0), (1, 0, 0), (0, -1, 0), (0, 1, 0), (0, 0, -1), (0, 0, 1))}
    for k, (head, tile) in enumerate(((ends[-1, 0, 0], 1), (own, 0), (own, 1), (ends[1, 0, 0], 0))):
        for n, which in enumerate((0, 3, 4)):
            cx[k, n] = jnp.broadcast_to(entry(head, tile, which), (16, 128))
    rows, lanes = iota((32, 128), 0), iota((16, 256), 1)
    for tile in range(2):
        for n, which in enumerate((3, 1, 5)):
            cy[tile, n] = jnp.where(
                rows == 7,
                entry(ends[0, -1, 0], tile, which),
                jnp.where(rows == 24, entry(ends[0, 1, 0], tile, which), entry(own, tile, which)),
            )
        for n, which in enumerate((4, 5, 2)):
            cz[tile, n] = jnp.where(
                lanes == 255,
                entry(ends[0, 0, -1], tile, which),
                jnp.where(lanes == 128, entry(ends[0, 0, 1], tile, which), entry(own, tile, which)),
            )
    return entry(own, 0, 6), entry(own, 1, 6)


def fill_extended(vext, v, faces, got, pos_ref, sizes):
    xm, xp, ym, yp, zm, zp = faces
    vext[2:18, 8:24, 0:128] = v[...]
    vext[0:2, 8:24, 0:128] = xm[...]
    vext[18:20, 8:24, 0:128] = xp[...]
    vext[2:18, 0:8, 0:128] = ym[...]
    vext[2:18, 24:32, 0:128] = yp[...]
    row, lane = iota((8, 128), 0), iota((8, 128), 1)
    place = ((row < 4) & (lane == jnp.where(row < 2, row + 126, row - 2))).astype(F32)
    outer = jnp.concatenate([zm[...], zp[...], jnp.zeros((4, 256), F32)], 0)
    beyond = lax.dot_general(outer, place, TN, precision=HIGHEST, preferred_element_type=F32)
    vext[2:18, 8:24, 128:256] = beyond.reshape(16, 16, 128)
    for dx, i in ((-1, 1), (1, 18)):
        for dy, j in ((-1, 7), (1, 24)):
            vext[i, j : j + 1, 0:128] = edges_of(pos_ref, sizes, got, (dx, dy, 0))
    lanes = iota((1, 128), 1)
    group = lanes // 16
    lines = []
    for dz in (-1, 1):
        line = jnp.zeros((1, 128), F32)
        for g, (dx, dy) in enumerate(((1, 0), (-1, 0), (0, 1), (0, -1))):
            line = jnp.where(group == g, edges_of(pos_ref, sizes, got, (dx, dy, dz)), line)
        lines.append(line)
    outer = jnp.concatenate([*lines, jnp.zeros((6, 128), F32)], 0)
    place = ((row < 2) & (lane == jnp.where(row == 0, 127, 0))).astype(F32)
    beyond = lax.dot_general(outer, place, TN, precision=HIGHEST, preferred_element_type=F32)
    vext[18, 8:24, 128:256] = beyond[0:16]
    vext[1, 8:24, 128:256] = beyond[16:32]
    for x in range(CX):
        vext[2 + x, 24:25, 128:256] = beyond[32 + x : 33 + x]
        vext[2 + x, 7:8, 128:256] = beyond[48 + x : 49 + x]


def flux_x(vext, fx, cx):
    def one(p, tile):
        wide = vext[p, 8:24, :]
        gx = vext[p + 1, 8:24, 0:128] - vext[p - 1, 8:24, 0:128]
        gy = vext[p, 9:25, 0:128] - vext[p, 7:23, 0:128]
        gz = (pltpu.roll(wide, 255, 1) - pltpu.roll(wide, 1, 1))[:, 0:128]
        fx[p - 1] = cx[tile, 0] * gx + cx[tile, 1] * gy + cx[tile, 2] * gz

    one(1, 0)
    one(18, 3)

    @pl.loop(2, 18, unroll=4)
    def _(p):
        one(p, jnp.where(p < 10, 1, 2))


def lap_plane(vext, fx, cy, cz, x):
    p = x + 2
    tile = x // 8
    wide = vext[p]
    gx = vext[p + 1] - vext[p - 1]
    gy = pltpu.roll(wide, 31, 0) - pltpu.roll(wide, 1, 0)
    gz = pltpu.roll(wide, 255, 1) - pltpu.roll(wide, 1, 1)
    fy = cy[tile, 0] * gx[:, 0:128] + cy[tile, 1] * gy[:, 0:128] + cy[tile, 2] * gz[:, 0:128]
    dy = (pltpu.roll(fy, 31, 0) - pltpu.roll(fy, 1, 0))[8:24]
    fz = cz[tile, 0] * gx[8:24] + cz[tile, 1] * gy[8:24] + cz[tile, 2] * gz[8:24]
    dz = (pltpu.roll(fz, 255, 1) - pltpu.roll(fz, 1, 1))[:, 0:128]
    return 0.25 * (fx[x + 2] - fx[x] + dy + dz)


def column_wide(values):
    return jnp.concatenate([jnp.broadcast_to(values[:, z : z + 1], (64, 256)) for z in range(4)], 0)


def to_row(wide):
    return jnp.sum(jnp.where(iota((256, 256), 0) == iota((256, 256), 1), wide, 0.0), axis=0, keepdims=True)


def first_kernel(sizes, pos_ref, act_ref, fi_ref, half_ref, slope_ref, tau_ref, cond_ref, rev_ref, angle, conduct, block_elem,
                 states, s1, xlo, xhi, ylo, yhi, zlo, zhi, msg, code_col, code_row, const, lines):
    gate_constants(half_ref, slope_ref, tau_ref, cond_ref, rev_ref, const)

    @pl.loop(0, CX)
    def _(x):
        alive = act_ref[x // 8, 0, 0] > 0
        s1[0, x] = ionic_plane(states[0, x], states, s1, x, alive, const)[0]

    ids = block_elem[...].reshape(64, 4)
    owner = column_wide((ids // ELEMS).astype(F32))
    local = column_wide((ids % ELEMS).astype(F32))
    owner_row = to_row(owner)
    before = iota((256, 256), 1) < iota((256, 256), 0)
    rank = jnp.sum(jnp.where((owner == owner_row) & before, 1.0, 0.0), axis=1, keepdims=True)
    code = owner + 256.0 * rank
    code_col[...] = code[:, 0:128]
    row_code = to_row(code)
    code_row[...] = jnp.broadcast_to(row_code, (8, 256))
    local_row = to_row(local) + 1.0
    peers = iota((256, 256), 0).astype(F32)
    lane = iota((1, 128), 1)
    a, b = frame_of(angle), conduct[...]
    spread = b[0:1] - b[1:2]
    entries = [b[1:2] + spread * a[n] * a[n] for n in range(3)]
    entries += [spread * a[0] * a[1], spread * a[0] * a[2], spread * a[1] * a[2]]
    head = jnp.zeros((1, 128), F32)
    slots = iota((1, NF), 1)
    for tile in range(2):
        alive = (act_ref[tile, 0, 0] > 0).astype(F32)
        chosen = slots == fi_ref[tile, 0, 0]
        for n in range(6):
            value = jnp.sum(jnp.where(chosen, entries[n], 0.0), axis=1, keepdims=True) * alive
            head = jnp.where(lane == HEAD + 7 * tile + n, value, head)
        head = jnp.where(lane == HEAD + 7 * tile + 6, alive, head)
    asked = jnp.broadcast_to(head, (256, 128))
    target = iota((128, 256), 0)
    for r in range(2):
        goes = (row_code == peers + 256.0 * r).astype(F32).astype(BF16)
        labels = jnp.where(target == r, local_row, 0.0).astype(BF16)
        asked += lax.dot_general(goes, labels, NT, preferred_element_type=F32)
    msg[:, 0:128] = asked
    msg[:, 128:256] = jnp.zeros((256, 128), F32)
    send_faces(s1.at[0], pos_ref, sizes, xlo, xhi, ylo, yhi, zlo, zhi, msg, lines)


def element_kernel(material, angle, node_disp, elem_node, elem_fibre, corner, passive, active):
    table = jnp.concatenate([*frame_of(angle), jnp.zeros((5, NF), F32)], 0)
    hot = (iota((NF, ELEMS), 0) == elem_fibre[...]).astype(F32)
    fibre = jnp.dot(table, hot, precision=HIGHEST, preferred_element_type=F32)
    f = [fibre[j : j + 1] for j in range(3)]
    disp = jnp.concatenate([node_disp[...], jnp.zeros((5, NODES), F32)], 0)
    packed = jnp.concatenate([p.astype(F32) for p in parts3(disp)] + [jnp.zeros((8, NODES), F32)], 0).astype(BF16)
    slope = [jnp.zeros((8, ELEMS), F32) for _ in range(3)]
    for q in range(8):
        hot = (iota((NODES, ELEMS), 0) == elem_node[q : q + 1, :]).astype(F32).astype(BF16)
        got = jnp.dot(packed, hot, preferred_element_type=F32)
        got = got[0:8] + got[8:16] + got[16:24]
        corner[8 * q : 8 * q + 8] = got
        for j in range(3):
            slope[j] += got if CORNERS[q][j] else -got
    F = [[slope[j][i : i + 1] * 0.25 + (1.0 if i == j else 0.0) for j in range(3)] for i in range(3)]

    def cofactor(i, j):
        a, b = [n for n in range(3) if n != i]
        c, d = [n for n in range(3) if n != j]
        minor = F[a][c] * F[b][d] - F[a][d] * F[b][c]
        return minor if (i + j) % 2 == 0 else -minor

    cof = [[cofactor(i, j) for j in range(3)] for i in range(3)]
    volume = F[0][0] * cof[0][0] + F[0][1] * cof[0][1] + F[0][2] * cof[0][2]
    invert = 1.0 / volume
    bulk = material[1] * jnp.log(volume)
    none = jnp.zeros((5, ELEMS), F32)
    stress, fibres = [], []
    stretch = [F[i][0] * f[0] + F[i][1] * f[1] + F[i][2] * f[2] for i in range(3)]
    for j in range(3):
        rows = []
        for i in range(3):
            inverse = cof[i][j] * invert
            rows.append(material[0] * (F[i][j] - inverse) + bulk * inverse)
        stress.append(jnp.concatenate([*rows, none], 0))
        fibres.append(jnp.concatenate([*[material[2] * stretch[i] * f[j] for i in range(3)], none], 0))
    total = jnp.zeros((24, NODES), F32)
    for q in range(8):
        sign = [0.25 if CORNERS[q][j] else -0.25 for j in range(3)]
        force = stress[0] * sign[0] + stress[1] * sign[1] + stress[2] * sign[2]
        active[8 * q : 8 * q + 8] = fibres[0] * sign[0] + fibres[1] * sign[1] + fibres[2] * sign[2]
        hot = (iota((NODES, ELEMS), 0) == elem_node[q : q + 1, :]).astype(F32).astype(BF16)
        packed = jnp.concatenate([p.astype(F32) for p in parts3(force)], 0).astype(BF16)
        total += lax.dot_general(packed, hot, NT, preferred_element_type=F32)
    passive[...] = total[0:8] + total[8:16] + total[16:24]


def second_kernel(sizes, pos_ref, half_ref, slope_ref, tau_ref, cond_ref, rev_ref, s1, xm, xp, ym, yp, zm, zp, got1, corner,
                  code_row, block_weight, s2, xlo, xhi, ylo, yhi, zlo, zhi, msg, const, lines, vext, fx, cx, cy, cz, tens):
    gate_constants(half_ref, slope_ref, tau_ref, cond_ref, rev_ref, const)
    live = tile_planes(pos_ref, sizes, got1, cx, cy, cz)
    fill_extended(vext, s1.at[0], (xm, xp, ym, yp, zm, zp), got1, pos_ref, sizes)
    flux_x(vext, fx, cx)

    @pl.loop(0, CX)
    def _(x):
        here = jnp.where(x < 8, live[0], live[1])
        volt = s1[0, x] + here * lap_plane(vext, fx, cy, cz, x)
        alive = jnp.broadcast_to(here, (16, 128)) > 0.5
        vstar, calcium = ionic_plane(volt, s1, s2, x, alive, const)
        s2[0, x] = vstar
        square = calcium * calcium
        tens[x] = square / (square + 0.09)

    pairs = jnp.concatenate([tens[2 * n] + tens[2 * n + 1] for n in range(8)], 0)
    row, lane = iota((64, 128), 0), iota((64, 128), 1)
    over_y = ((row // 8 == lane // 16) & (row % 8 == lane % 16 // 2)).astype(F32)
    over_z = jnp.where(iota((128, 128), 0) // 32 == iota((128, 128), 1), 1.0 / 128.0, 0.0)
    mean = jnp.dot(over_y, pairs, precision=HIGHEST, preferred_element_type=F32)
    mean = jnp.dot(mean, over_z, precision=HIGHEST, preferred_element_type=F32)
    value = to_row(column_wide(mean[:, 0:4] * block_weight[...].reshape(64, 4)))
    peers = iota((256, 256), 0).astype(F32)
    elems = iota((256, 256), 1).astype(F32)
    target = iota((128, 256), 0)
    answer = jnp.zeros((256, 128), F32)
    none = jnp.zeros((64, 256), F32)
    for r in range(2):
        goes = (code_row[0:1, :] == peers + 256.0 * r).astype(F32).astype(BF16)
        for part in parts3(jnp.where(target == 64 * r + 3, value, 0.0)):
            answer += lax.dot_general(goes, part, NT, preferred_element_type=F32)
        wants = (got1[:, r : r + 1] == elems + 1.0).astype(F32).astype(BF16)
        held = jnp.concatenate([corner[...], none] if r == 0 else [none, corner[...]], 0)
        for part in parts3(held):
            answer += lax.dot_general(wants, part, NT, preferred_element_type=F32)
    msg[:, 0:128] = answer
    msg[:, 128:256] = jnp.zeros((256, 128), F32)
    send_faces(s2.at[0], pos_ref, sizes, xlo, xhi, ylo, yhi, zlo, zhi, msg, lines)


def third_kernel(sizes, pos_ref, s2, xm, xp, ym, yp, zm, zp, got1, got2, code_col, elem_node, passive, active, blend, s3, fine,
                 residual, vext, fx, cx, cy, cz):
    live = tile_planes(pos_ref, sizes, got1, cx, cy, cz)
    fill_extended(vext, s2.at[0], (xm, xp, ym, yp, zm, zp), got2, pos_ref, sizes)
    flux_x(vext, fx, cx)

    @pl.loop(0, CX)
    def _(x):
        here = jnp.where(x < 8, live[0], live[1])
        s3[0, x] = s2[0, x] + here * lap_plane(vext, fx, cy, cz, x)

    elems = iota((256, 256), 1).astype(F32)
    tension = jnp.zeros((1, 256), F32)
    for r in range(2):
        wants = got1[:, r : r + 1] == elems + 1.0
        tension += jnp.sum(jnp.where(wants, got2[:, 64 * r + 3 : 64 * r + 4], 0.0), axis=0, keepdims=True)
    total = jnp.zeros((24, NODES), F32)
    for q in range(8):
        hot = (iota((NODES, ELEMS), 0) == elem_node[q : q + 1, :]).astype(F32).astype(BF16)
        packed = jnp.concatenate([p.astype(F32) for p in parts3(active[8 * q : 8 * q + 8] * tension)], 0).astype(BF16)
        total += lax.dot_general(packed, hot, NT, preferred_element_type=F32)
    total = passive[...] + total[0:8] + total[8:16] + total[16:24]
    residual[...] = total[0:3]

    code = jnp.concatenate([code_col[...], code_col[...]], 1)
    answer = got2[:, 0:128]
    lane = iota((256, 128), 1)
    disp = jnp.zeros((256, 128), F32)
    for r in range(2):
        goes = (code == elems + 256.0 * r).astype(F32).astype(BF16)
        part = jnp.where(lane // 64 == r, answer, 0.0)
        part = part if r == 0 else pltpu.roll(part, 64, 1)
        for piece in parts3(part):
            disp += jnp.dot(goes, piece, preferred_element_type=F32)
    merged = jnp.concatenate(
        [disp[0:64] + pltpu.roll(disp[64:128], 64, 1), disp[128:192] + pltpu.roll(disp[192:256], 64, 1)], 1
    )
    which = iota((64, 256), 1) % 8
    rows = jnp.concatenate([jnp.where(which == c, merged, 0.0) for c in range(3)], 0)
    first, second, third = parts3(rows)
    out = jnp.dot(first, blend[0], preferred_element_type=F32) + jnp.dot(second, blend[0], preferred_element_type=F32)
    out += jnp.dot(first, blend[1], preferred_element_type=F32)
    for c in range(3):
        for bx in range(8):
            tile = out[64 * c + 8 * bx : 64 * c + 8 * bx + 8]
            for i in range(2):
                for j in range(2):
                    at = 128 * (2 * i + j)
                    fine[c, 2 * bx + i, pl.ds(j, 8, stride=2), :] = tile[:, at : at + 128]


def blend_table():
    table = np.zeros((4, 8, 8, 2, 2, 128), np.float64)
    z = np.arange(128)
    for q, bits in enumerate(CORNERS):
        for i in range(2):
            for j in range(2):
                for bz in range(4):
                    xi = ((i + 0.5) / 2, (j + 0.5) / 2, (z % 32 + 0.5) / 32)
                    w = 1.0
                    for d in range(3):
                        w = w * (xi[d] if bits[d] else 1.0 - xi[d])
                    table[bz, q, :, i, j] = w * (z // 32 == bz)
    table = table.reshape(256, 512)
    import ml_dtypes

    first = table.astype(ml_dtypes.bfloat16)
    second = (table - first.astype(np.float64)).astype(ml_dtypes.bfloat16)
    return np.stack([first, second])


def shift(x, axis, by):
    count = lax.axis_size(axis)
    pairs = [(i, i + by) for i in range(count) if 0 <= i + by < count]
    return lax.ppermute(x, axis, pairs)


def exchange(xlo, xhi, ylo, yhi, zlo, zhi, msg):
    got = lax.all_to_all(msg.reshape(256, 1, 256), ALL, 0, 0, tiled=True).reshape(256, 256)
    return (
        shift(xhi, "gx", 1),
        shift(xlo, "gx", -1),
        shift(yhi, "gy", 1),
        shift(ylo, "gy", -1),
        shift(zhi, "gz", 1),
        shift(zlo, "gz", -1),
    ), got


SMEM = pl.BlockSpec(memory_space=pltpu.SMEM)
VMEM = pl.BlockSpec(memory_space=pltpu.VMEM)


def sds(*shape):
    return jax.ShapeDtypeStruct(shape, F32)


FACES = [sds(2, 16, 128), sds(2, 16, 128), sds(16, 8, 128), sds(16, 8, 128), sds(2, 256), sds(2, 256), sds(256, 256)]
STEP_SCRATCH = [
    pltpu.VMEM((20, 32, 256), F32),
    pltpu.VMEM((18, 16, 128), F32),
    pltpu.VMEM((4, 3, 16, 128), F32),
    pltpu.VMEM((2, 3, 32, 128), F32),
    pltpu.VMEM((2, 3, 16, 256), F32),
]
GATE_SCRATCH = [pltpu.VMEM((6 * NCH, 8, 128), F32), pltpu.VMEM((128, 128), F32)]
PARAMS = pltpu.CompilerParams(vmem_limit_bytes=40 * 2**20)


def shards(states, active, fibre_index, fibre_angle, conduct, gate_half, gate_slope, gate_tau, conductance, reversal,
           block_elem, block_weight, node_disp, elem_node, elem_fibre, material):
    sizes = tuple(lax.axis_size(a) for a in ALL)
    pos = jnp.stack([lax.axis_index(a) for a in ALL]).astype(jnp.int32)
    gates = (gate_half, gate_slope, gate_tau, conductance, reversal)
    full = sds(NSTATE, CX, CY, CZ)
    s1, *faces, code_col, code_row = pl.pallas_call(
        functools.partial(first_kernel, sizes),
        out_shape=[full, *FACES, sds(256, 128), sds(8, 256)],
        in_specs=[SMEM] * 8 + [VMEM] * 4,
        out_specs=[VMEM] * 10,
        scratch_shapes=GATE_SCRATCH,
        compiler_params=PARAMS,
        name="first",
    )(pos, active, fibre_index, *gates, fibre_angle, conduct, block_elem, states)
    halo, got1 = exchange(*faces)
    corner, passive, active_force = pl.pallas_call(
        element_kernel,
        out_shape=[sds(64, ELEMS), sds(8, NODES), sds(64, ELEMS)],
        in_specs=[SMEM] + [VMEM] * 4,
        out_specs=[VMEM] * 3,
        compiler_params=PARAMS,
        name="elements",
    )(material, fibre_angle, node_disp, elem_node, elem_fibre.reshape(1, ELEMS))
    s2, *faces = pl.pallas_call(
        functools.partial(second_kernel, sizes),
        out_shape=[full, *FACES],
        in_specs=[SMEM] * 6 + [VMEM] * 11,
        out_specs=[VMEM] * 8,
        scratch_shapes=GATE_SCRATCH + STEP_SCRATCH + [pltpu.VMEM((16, 16, 128), F32)],
        compiler_params=PARAMS,
        name="second",
    )(pos, *gates, s1, *halo, got1, corner, code_row, block_weight)
    halo, got2 = exchange(*faces)
    plane = pl.BlockSpec((1, CX, CY, CZ), lambda i: (0, 0, 0, 0))

    def whole(x):
        return pl.BlockSpec(x.shape, lambda i: (0,) * x.ndim)

    blend = jnp.asarray(blend_table())
    rest = (*halo, got1, got2, code_col, elem_node, passive, active_force, blend)
    outs = [full, sds(3, CX, CY, CZ), sds(3, NODES)]
    return pl.pallas_call(
        functools.partial(third_kernel, sizes),
        grid=(1,),
        out_shape=outs,
        in_specs=[SMEM, plane, *[whole(x) for x in rest]],
        out_specs=[plane, whole(outs[1]), whole(outs[2])],
        scratch_shapes=STEP_SCRATCH,
        input_output_aliases={1: 0},
        compiler_params=PARAMS,
        name="third",
    )(pos, s2, *rest)


def solution(mesh):
    in_specs = (
        P(None, "gx", "gy", "gz"),
        *[P("gx", "gy", "gz")] * 2,
        *[P()] * 7,
        *[P("gx", "gy", "gz")] * 2,
        *[P(None, ALL)] * 2,
        P(ALL),
        P(),
    )
    out_specs = (P(None, "gx", "gy", "gz"), P(None, "gx", "gy", "gz"), P(None, ALL))
    return jax.shard_map(shards, mesh=mesh, in_specs=in_specs, out_specs=out_specs, check_vma=False)
```

```python
import functools

import jax
import jax.numpy as jnp
import numpy as np
from jax import lax
from jax.experimental import pallas as pl
from jax.experimental.pallas import tpu as pltpu
from jax.sharding import PartitionSpec as P

NSTATE, NCH, NF = 19, 17, 64
CX, CY, CZ = 16, 16, 128
ELEMS, SLOTS, NODES = 256, 256, 512
ALL = ("gx", "gy", "gz")
HIGHEST = lax.Precision.HIGHEST
F32, BF16 = jnp.float32, jnp.bfloat16
NT = (((1,), (1,)), ((), ()))
TN = (((0,), (0,)), ((), ()))
CORNERS = [(q // 4, q // 2 % 2, q % 2) for q in range(8)]
HEAD = 2


def iota(shape, dim):
    return lax.broadcasted_iota(jnp.int32, shape, dim)


def neighbour(pos_ref, sizes, step):
    at = [pos_ref[d] + step[d] for d in range(3)]
    ok = (at[0] >= 0) & (at[0] < sizes[0])
    for d in (1, 2):
        ok = ok & (at[d] >= 0) & (at[d] < sizes[d])
    row = (at[0] * sizes[1] + at[1]) * sizes[2] + at[2]
    return jnp.where(ok, row, 0), ok


ROWS = 5
FIRST = pl.ds(0, 256, stride=ROWS)


def put_row(msg, peer, ok, values, place=1):
    row = ROWS * peer + place
    base = pl.ds(pl.multiple_of(row // 8 * 8, 8), 8)
    here = iota((8, 128), 0) == jnp.where(ok, row % 8, -1)
    msg[base, :] = jnp.where(here, values, msg[base, :])


def take_row(got, peer, ok, place):
    row = ROWS * peer + place
    rows = got[pl.ds(pl.multiple_of(row // 8 * 8, 8), 8), :]
    here = iota((8, 128), 0) == jnp.where(ok, row % 8, -1)
    return jnp.sum(jnp.where(here, rows, 0.0), axis=0, keepdims=True)


def parts3(x):
    first = x.astype(BF16)
    rest = x - first.astype(F32)
    second = rest.astype(BF16)
    third = (rest - second.astype(F32)).astype(BF16)
    return first, second, third


def frame_of(angles):
    a, b = angles[0:1, :], angles[1:2, :]
    return jnp.cos(a) * jnp.cos(b), jnp.sin(a) * jnp.cos(b), jnp.sin(b)


def gate_constants(half_ref, slope_ref, tau_ref, cond_ref, rev_ref, const):
    for c in range(NCH):
        scale = 0.5 / jnp.full((8, 128), slope_ref[c], F32)
        keep = jnp.exp(-1.0 / jnp.full((8, 128), tau_ref[c], F32))
        cond = jnp.full((8, 128), cond_ref[c], F32)
        const[c] = scale
        const[NCH + c] = -half_ref[c] * scale
        const[2 * NCH + c] = keep
        const[3 * NCH + c] = 0.5 * (1.0 - keep)
        const[4 * NCH + c] = cond
        const[5 * NCH + c] = cond * rev_ref[c]


def twice(x):
    return jnp.concatenate([x, x], 0)


def ionic_plane(volt, source, target, x, alive, const):
    total = jnp.zeros_like(volt)
    moment = jnp.zeros_like(volt)
    for c in range(NCH):
        rise = jnp.tanh(volt * twice(const[c]) + twice(const[NCH + c]))
        old = source[1 + c, x]
        lift = twice(const[3 * NCH + c])
        gate = old * twice(const[2 * NCH + c]) + (lift * rise + lift)
        total += gate * twice(const[4 * NCH + c])
        moment += gate * twice(const[5 * NCH + c])
        target[1 + c, x] = jnp.where(alive, gate, old)
    vstar = volt - (volt * total - moment)
    old = source[NSTATE - 1, x]
    calcium = old * 0.9 + 0.1 * (0.5 * jnp.tanh(4.0 * (volt - 0.5)) + 0.5)
    calcium = jnp.where(alive, calcium, old)
    target[NSTATE - 1, x] = calcium
    return jnp.where(alive, vstar, volt), calcium


def send_faces(v, pos_ref, sizes, xlo, xhi, ylo, yhi, msg, lines):
    xlo[...] = v[0:2]
    xhi[...] = v[14:16]
    ylo[...] = v[:, 0:8, :]
    yhi[...] = v[:, 8:16, :]
    row, lane = iota((8, 128), 0), iota((8, 128), 1)
    pick = ((row < 4) & (lane == jnp.where(row < 2, row, row + 124))).astype(F32)
    flat = v[...].reshape(CX * CY, CZ)
    ends = lax.dot_general(pick, flat, NT, precision=HIGHEST, preferred_element_type=F32)
    for dz in (-1, 1):
        peer, ok = neighbour(pos_ref, sizes, (0, 0, dz))
        for n in range(4):
            k, half = n // 2 + (2 if dz > 0 else 0), n % 2
            put_row(msg, peer, ok, ends[k : k + 1, 128 * half : 128 * half + 128], 1 + n)
    lines[0:16] = v[0]
    lines[16:32] = v[15]
    for x in range(CX):
        lines[32 + x : 33 + x] = v[x, 0:1, :]
        lines[48 + x : 49 + x] = v[x, 15:16, :]
    lines[64:128] = jnp.zeros((64, 128), F32)
    marks = lax.dot_general(pick, lines[...], NT, precision=HIGHEST, preferred_element_type=F32)
    for dx in (-1, 1):
        for dy in (-1, 1):
            peer, ok = neighbour(pos_ref, sizes, (dx, dy, 0))
            edge = v[15 if dx > 0 else 0, (15 if dy > 0 else 0) : (16 if dy > 0 else 1), :]

            put_row(msg, peer, ok, edge)

    for step in ((-1, 0), (1, 0), (0, -1), (0, 1)):
        for dz in (-1, 1):
            peer, ok = neighbour(pos_ref, sizes, (*step, dz))
            edge = marks[3:4] if dz > 0 else marks[0:1]

            put_row(msg, peer, ok, edge)


def heads(pos_ref, sizes, got, step):
    row, ok = neighbour(pos_ref, sizes, step)
    return take_row(got, row, ok, 0)


def entry(head, tile, which):
    lane = HEAD + 7 * tile + which
    return head[:, lane : lane + 1]


def edges_of(pos_ref, sizes, got, step):
    row, ok = neighbour(pos_ref, sizes, step)
    return take_row(got, row, ok, 1)


def tile_planes(pos_ref, sizes, got1, cx, cy, cz):
    own = heads(pos_ref, sizes, got1, (0, 0, 0))
    ends = {s: heads(pos_ref, sizes, got1, s) for s in ((-1, 0, 0), (1, 0, 0), (0, -1, 0), (0, 1, 0), (0, 0, -1), (0, 0, 1))}
    for k, (head, tile) in enumerate(((ends[-1, 0, 0], 1), (own, 0), (own, 1), (ends[1, 0, 0], 0))):
        for n, which in enumerate((0, 3, 4)):
            cx[k, n] = jnp.broadcast_to(entry(head, tile, which), (16, 128))
    rows, lanes = iota((32, 128), 0), iota((16, 256), 1)
    for tile in range(2):
        for n, which in enumerate((3, 1, 5)):
            cy[tile, n] = jnp.where(
                rows == 7,
                entry(ends[0, -1, 0], tile, which),
                jnp.where(rows == 24, entry(ends[0, 1, 0], tile, which), entry(own, tile, which)),
            )
        for n, which in enumerate((4, 5, 2)):
            cz[tile, n] = jnp.where(
                lanes == 255,
                entry(ends[0, 0, -1], tile, which),
                jnp.where(lanes == 128, entry(ends[0, 0, 1], tile, which), entry(own, tile, which)),
            )
    return entry(own, 0, 6), entry(own, 1, 6)


def fill_extended(vext, v, faces, got, pos_ref, sizes):
    xm, xp, ym, yp = faces
    vext[2:18, 8:24, 0:128] = v[...]
    vext[0:2, 8:24, 0:128] = xm[...]
    vext[18:20, 8:24, 0:128] = xp[...]
    vext[2:18, 0:8, 0:128] = ym[...]
    vext[2:18, 24:32, 0:128] = yp[...]
    row, lane = iota((8, 128), 0), iota((8, 128), 1)
    place = ((row < 4) & (lane == jnp.where(row < 2, row + 126, row - 2))).astype(F32)
    outer = []
    for dz in (-1, 1):
        peer, ok = neighbour(pos_ref, sizes, (0, 0, dz))
        for k in range(2):
            outer.append(jnp.concatenate([take_row(got, peer, ok, 1 + 2 * k + half) for half in range(2)], 1))
    outer = jnp.concatenate([*outer, jnp.zeros((4, 256), F32)], 0)
    beyond = lax.dot_general(outer, place, TN, precision=HIGHEST, preferred_element_type=F32)
    vext[2:18, 8:24, 128:256] = beyond.reshape(16, 16, 128)
    for dx, i in ((-1, 1), (1, 18)):
        for dy, j in ((-1, 7), (1, 24)):
            vext[i, j : j + 1, 0:128] = edges_of(pos_ref, sizes, got, (dx, dy, 0))
    lanes = iota((1, 128), 1)
    group = lanes // 16
    lines = []
    for dz in (-1, 1):
        line = jnp.zeros((1, 128), F32)
        for g, (dx, dy) in enumerate(((1, 0), (-1, 0), (0, 1), (0, -1))):
            line = jnp.where(group == g, edges_of(pos_ref, sizes, got, (dx, dy, dz)), line)
        lines.append(line)
    outer = jnp.concatenate([*lines, jnp.zeros((6, 128), F32)], 0)
    place = ((row < 2) & (lane == jnp.where(row == 0, 127, 0))).astype(F32)
    beyond = lax.dot_general(outer, place, TN, precision=HIGHEST, preferred_element_type=F32)
    vext[18, 8:24, 128:256] = beyond[0:16]
    vext[1, 8:24, 128:256] = beyond[16:32]
    for x in range(CX):
        vext[2 + x, 24:25, 128:256] = beyond[32 + x : 33 + x]
        vext[2 + x, 7:8, 128:256] = beyond[48 + x : 49 + x]


def flux_x(vext, fx, cx):
    def one(p, tile):
        wide = vext[p, 8:24, :]
        gx = vext[p + 1, 8:24, 0:128] - vext[p - 1, 8:24, 0:128]
        gy = vext[p, 9:25, 0:128] - vext[p, 7:23, 0:128]
        gz = (pltpu.roll(wide, 255, 1) - pltpu.roll(wide, 1, 1))[:, 0:128]
        fx[p - 1] = cx[tile, 0] * gx + cx[tile, 1] * gy + cx[tile, 2] * gz

    one(1, 0)
    one(18, 3)

    @pl.loop(2, 18, unroll=4)
    def _(p):
        one(p, jnp.where(p < 10, 1, 2))


def lap_plane(vext, fx, cy, cz, x):
    p = x + 2
    tile = x // 8
    wide = vext[p]
    gx = vext[p + 1] - vext[p - 1]
    gy = pltpu.roll(wide, 31, 0) - pltpu.roll(wide, 1, 0)
    gz = pltpu.roll(wide, 255, 1) - pltpu.roll(wide, 1, 1)
    fy = cy[tile, 0] * gx[:, 0:128] + cy[tile, 1] * gy[:, 0:128] + cy[tile, 2] * gz[:, 0:128]
    dy = (pltpu.roll(fy, 31, 0) - pltpu.roll(fy, 1, 0))[8:24]
    fz = cz[tile, 0] * gx[8:24] + cz[tile, 1] * gy[8:24] + cz[tile, 2] * gz[8:24]
    dz = (pltpu.roll(fz, 255, 1) - pltpu.roll(fz, 1, 1))[:, 0:128]
    return 0.25 * (fx[x + 2] - fx[x] + dy + dz)


def blocks(ref):
    return jnp.concatenate([ref[n].T for n in range(8)], 0)


def column_wide(values):
    return jnp.concatenate([jnp.broadcast_to(values[:, z : z + 1], (64, 256)) for z in range(4)], 0)


def to_row(wide):
    return jnp.sum(jnp.where(iota((256, 256), 0) == iota((256, 256), 1), wide, 0.0), axis=0, keepdims=True)


def first_kernel(sizes, pos_ref, act_ref, fi_ref, half_ref, slope_ref, tau_ref, cond_ref, rev_ref, angle, conduct, block_elem,
                 states, s1, xlo, xhi, ylo, yhi, msg, code_col, code_row, const, lines):
    gate_constants(half_ref, slope_ref, tau_ref, cond_ref, rev_ref, const)

    @pl.loop(0, CX, unroll=2)
    def _(x):
        alive = act_ref[x // 8] > 0
        s1[0, x] = ionic_plane(states[0, x], states, s1, x, alive, const)[0]

    ids = blocks(block_elem)
    owner = column_wide((ids // ELEMS).astype(F32))
    local = column_wide((ids % ELEMS).astype(F32))
    owner_row = to_row(owner)
    before = iota((256, 256), 1) < iota((256, 256), 0)
    rank = jnp.sum(jnp.where((owner == owner_row) & before, 1.0, 0.0), axis=1, keepdims=True)
    code = owner + 256.0 * rank
    code_col[...] = code[:, 0:128]
    row_code = to_row(code)
    code_row[...] = jnp.broadcast_to(row_code, (8, 256))
    local_row = to_row(local) + 1.0
    peers = iota((256, 256), 0).astype(F32)
    lane = iota((1, 128), 1)
    a, b = frame_of(angle), conduct[...]
    spread = b[0:1] - b[1:2]
    entries = [b[1:2] + spread * a[n] * a[n] for n in range(3)]
    entries += [spread * a[0] * a[1], spread * a[0] * a[2], spread * a[1] * a[2]]
    head = jnp.zeros((1, 128), F32)
    slots = iota((1, NF), 1)
    for tile in range(2):
        alive = (act_ref[tile] > 0).astype(F32)
        chosen = slots == fi_ref[tile]
        for n in range(6):
            value = jnp.sum(jnp.where(chosen, entries[n], 0.0), axis=1, keepdims=True) * alive
            head = jnp.where(lane == HEAD + 7 * tile + n, value, head)
        head = jnp.where(lane == HEAD + 7 * tile + 6, alive, head)
    asked = jnp.broadcast_to(head, (256, 128))
    target = iota((128, 256), 0)
    for r in range(2):
        goes = (row_code == peers + 256.0 * r).astype(F32).astype(BF16)
        labels = jnp.where(target == r, local_row, 0.0).astype(BF16)
        asked += lax.dot_general(goes, labels, NT, preferred_element_type=F32)
    msg[...] = jnp.zeros((ROWS * 256, 128), F32)
    msg[FIRST, :] = asked
    send_faces(s1.at[0], pos_ref, sizes, xlo, xhi, ylo, yhi, msg, lines)


def element_kernel(material, angle, node_disp, elem_node, elem_fibre, corner, passive, active):
    table = jnp.concatenate([*frame_of(angle), jnp.zeros((5, NF), F32)], 0)
    hot = (iota((NF, ELEMS), 0) == elem_fibre[...]).astype(F32)
    fibre = jnp.dot(table, hot, precision=HIGHEST, preferred_element_type=F32)
    f = [fibre[j : j + 1] for j in range(3)]
    disp = jnp.concatenate([node_disp[...], jnp.zeros((5, NODES), F32)], 0)
    packed = jnp.concatenate([p.astype(F32) for p in parts3(disp)] + [jnp.zeros((8, NODES), F32)], 0).astype(BF16)
    slope = [jnp.zeros((8, ELEMS), F32) for _ in range(3)]
    for q in range(8):
        hot = (iota((NODES, ELEMS), 0) == elem_node[q : q + 1, :]).astype(F32).astype(BF16)
        got = jnp.dot(packed, hot, preferred_element_type=F32)
        got = got[0:8] + got[8:16] + got[16:24]
        corner[8 * q : 8 * q + 8] = got
        for j in range(3):
            slope[j] += got if CORNERS[q][j] else -got
    F = [[slope[j][i : i + 1] * 0.25 + (1.0 if i == j else 0.0) for j in range(3)] for i in range(3)]

    def cofactor(i, j):
        a, b = [n for n in range(3) if n != i]
        c, d = [n for n in range(3) if n != j]
        minor = F[a][c] * F[b][d] - F[a][d] * F[b][c]
        return minor if (i + j) % 2 == 0 else -minor

    cof = [[cofactor(i, j) for j in range(3)] for i in range(3)]
    volume = F[0][0] * cof[0][0] + F[0][1] * cof[0][1] + F[0][2] * cof[0][2]
    invert = 1.0 / volume
    bulk = material[1] * jnp.log(volume)
    none = jnp.zeros((5, ELEMS), F32)
    stress, fibres = [], []
    stretch = [F[i][0] * f[0] + F[i][1] * f[1] + F[i][2] * f[2] for i in range(3)]
    for j in range(3):
        rows = []
        for i in range(3):
            inverse = cof[i][j] * invert
            rows.append(material[0] * (F[i][j] - inverse) + bulk * inverse)
        stress.append(jnp.concatenate([*rows, none], 0))
        fibres.append(jnp.concatenate([*[material[2] * stretch[i] * f[j] for i in range(3)], none], 0))
    total = jnp.zeros((24, NODES), F32)
    for q in range(8):
        sign = [0.25 if CORNERS[q][j] else -0.25 for j in range(3)]
        force = stress[0] * sign[0] + stress[1] * sign[1] + stress[2] * sign[2]
        active[8 * q : 8 * q + 8] = fibres[0] * sign[0] + fibres[1] * sign[1] + fibres[2] * sign[2]
        hot = (iota((NODES, ELEMS), 0) == elem_node[q : q + 1, :]).astype(F32).astype(BF16)
        packed = jnp.concatenate([p.astype(F32) for p in parts3(force)], 0).astype(BF16)
        total += lax.dot_general(packed, hot, NT, preferred_element_type=F32)
    passive[...] = total[0:8] + total[8:16] + total[16:24]


def second_kernel(sizes, pos_ref, half_ref, slope_ref, tau_ref, cond_ref, rev_ref, s1, xm, xp, ym, yp, got1, corner,
                  code_row, block_weight, s2, xlo, xhi, ylo, yhi, msg, const, lines, vext, fx, cx, cy, cz, tens):
    gate_constants(half_ref, slope_ref, tau_ref, cond_ref, rev_ref, const)
    live = tile_planes(pos_ref, sizes, got1, cx, cy, cz)
    fill_extended(vext, s1.at[0], (xm, xp, ym, yp), got1, pos_ref, sizes)
    flux_x(vext, fx, cx)

    @pl.loop(0, CX, unroll=4)
    def _(x):
        here = jnp.where(x < 8, live[0], live[1])
        tens[x] = s1[0, x] + here * lap_plane(vext, fx, cy, cz, x)

    @pl.loop(0, CX, unroll=2)
    def _(x):
        here = jnp.where(x < 8, live[0], live[1])
        volt = tens[x]
        alive = jnp.broadcast_to(here, (16, 128)) > 0.5
        vstar, calcium = ionic_plane(volt, s1, s2, x, alive, const)
        s2[0, x] = vstar
        square = calcium * calcium
        tens[x] = square / (square + 0.09)

    pairs = jnp.concatenate([tens[2 * n] + tens[2 * n + 1] for n in range(8)], 0)
    row, lane = iota((64, 128), 0), iota((64, 128), 1)
    over_y = ((row // 8 == lane // 16) & (row % 8 == lane % 16 // 2)).astype(F32)
    over_z = jnp.where(iota((128, 128), 0) // 32 == iota((128, 128), 1), 1.0 / 128.0, 0.0)
    mean = jnp.dot(over_y, pairs, precision=HIGHEST, preferred_element_type=F32)
    mean = jnp.dot(mean, over_z, precision=HIGHEST, preferred_element_type=F32)
    value = to_row(column_wide(mean[:, 0:4] * blocks(block_weight)))
    peers = iota((256, 256), 0).astype(F32)
    elems = iota((256, 256), 1).astype(F32)
    target = iota((128, 256), 0)
    answer = jnp.zeros((256, 128), F32)
    asked = got1[FIRST, :]
    none = jnp.zeros((64, 256), F32)
    for r in range(2):
        goes = (code_row[0:1, :] == peers + 256.0 * r).astype(F32).astype(BF16)
        for part in parts3(jnp.where(target == 64 * r + 3, value, 0.0)):
            answer += lax.dot_general(goes, part, NT, preferred_element_type=F32)
        wants = (asked[:, r : r + 1] == elems + 1.0).astype(F32).astype(BF16)
        held = jnp.concatenate([corner[...], none] if r == 0 else [none, corner[...]], 0)
        for part in parts3(held):
            answer += lax.dot_general(wants, part, NT, preferred_element_type=F32)
    msg[...] = jnp.zeros((ROWS * 256, 128), F32)
    msg[FIRST, :] = answer
    send_faces(s2.at[0], pos_ref, sizes, xlo, xhi, ylo, yhi, msg, lines)


def third_kernel(sizes, pos_ref, s2, xm, xp, ym, yp, got1, got2, code_col, elem_node, passive, active, blend, s3, fine,
                 residual, vext, fx, cx, cy, cz):
    live = tile_planes(pos_ref, sizes, got1, cx, cy, cz)
    fill_extended(vext, s2.at[0], (xm, xp, ym, yp), got2, pos_ref, sizes)
    flux_x(vext, fx, cx)

    @pl.loop(0, CX, unroll=4)
    def _(x):
        here = jnp.where(x < 8, live[0], live[1])
        s3[0, x] = s2[0, x] + here * lap_plane(vext, fx, cy, cz, x)

    elems = iota((256, 256), 1).astype(F32)
    tension = jnp.zeros((1, 256), F32)
    asked, answer = got1[FIRST, :], got2[FIRST, :]
    for r in range(2):
        wants = asked[:, r : r + 1] == elems + 1.0
        tension += jnp.sum(jnp.where(wants, answer[:, 64 * r + 3 : 64 * r + 4], 0.0), axis=0, keepdims=True)
    total = jnp.zeros((24, NODES), F32)
    for q in range(8):
        hot = (iota((NODES, ELEMS), 0) == elem_node[q : q + 1, :]).astype(F32).astype(BF16)
        packed = jnp.concatenate([p.astype(F32) for p in parts3(active[8 * q : 8 * q + 8] * tension)], 0).astype(BF16)
        total += lax.dot_general(packed, hot, NT, preferred_element_type=F32)
    total = passive[...] + total[0:8] + total[8:16] + total[16:24]
    residual[...] = total[0:3]

    code = jnp.concatenate([code_col[...], code_col[...]], 1)
    lane = iota((256, 128), 1)
    disp = jnp.zeros((256, 128), F32)
    for r in range(2):
        goes = (code == elems + 256.0 * r).astype(F32).astype(BF16)
        part = jnp.where(lane // 64 == r, answer, 0.0)
        part = part if r == 0 else pltpu.roll(part, 64, 1)
        for piece in parts3(part):
            disp += jnp.dot(goes, piece, preferred_element_type=F32)
    merged = jnp.concatenate(
        [disp[0:64] + pltpu.roll(disp[64:128], 64, 1), disp[128:192] + pltpu.roll(disp[192:256], 64, 1)], 1
    )
    which = iota((64, 256), 1) % 8
    rows = jnp.concatenate([jnp.where(which == c, merged, 0.0) for c in range(3)], 0)
    first, second, third = parts3(rows)
    out = jnp.dot(first, blend[0], preferred_element_type=F32) + jnp.dot(second, blend[0], preferred_element_type=F32)
    out += jnp.dot(first, blend[1], preferred_element_type=F32)
    for c in range(3):
        for bx in range(8):
            tile = out[64 * c + 8 * bx : 64 * c + 8 * bx + 8]
            for i in range(2):
                for j in range(2):
                    at = 128 * (2 * i + j)
                    fine[c, 2 * bx + i, pl.ds(j, 8, stride=2), :] = tile[:, at : at + 128]


def blend_table():
    table = np.zeros((4, 8, 8, 2, 2, 128), np.float64)
    z = np.arange(128)
    for q, bits in enumerate(CORNERS):
        for i in range(2):
            for j in range(2):
                for bz in range(4):
                    xi = ((i + 0.5) / 2, (j + 0.5) / 2, (z % 32 + 0.5) / 32)
                    w = 1.0
                    for d in range(3):
                        w = w * (xi[d] if bits[d] else 1.0 - xi[d])
                    table[bz, q, :, i, j] = w * (z // 32 == bz)
    table = table.reshape(256, 512)
    import ml_dtypes

    first = table.astype(ml_dtypes.bfloat16)
    second = (table - first.astype(np.float64)).astype(ml_dtypes.bfloat16)
    return np.stack([first, second])


def shift(x, axis, by):
    count = lax.axis_size(axis)
    pairs = [(i, i + by) for i in range(count) if 0 <= i + by < count]
    return lax.ppermute(x, axis, pairs)


def exchange(xlo, xhi, ylo, yhi, msg):
    got = lax.all_to_all(msg.reshape(256, 1, ROWS * 128), ALL, 0, 0, tiled=True).reshape(ROWS * 256, 128)
    halo = shift(xhi, "gx", 1), shift(xlo, "gx", -1), shift(yhi, "gy", 1), shift(ylo, "gy", -1)
    return halo, got


def whole(shape, space=None):
    return pl.BlockSpec(shape, lambda i: (0,) * len(shape), memory_space=space)


def call(body, name, scalars, arrays, outs, scratch=(), **more):
    return pl.pallas_call(
        body,
        grid=(1,),
        out_shape=outs,
        in_specs=[whole(x.shape, pltpu.SMEM) for x in scalars] + [whole(x.shape) for x in arrays],
        out_specs=[whole(x.shape) for x in outs],
        scratch_shapes=scratch,
        compiler_params=PARAMS,
        name=name,
        **more,
    )(*scalars, *arrays)


def sds(*shape):
    return jax.ShapeDtypeStruct(shape, F32)


FACES = [sds(2, 16, 128), sds(2, 16, 128), sds(16, 8, 128), sds(16, 8, 128), sds(ROWS * 256, 128)]
STEP_SCRATCH = [
    pltpu.VMEM((20, 32, 256), F32),
    pltpu.VMEM((18, 16, 128), F32),
    pltpu.VMEM((4, 3, 16, 128), F32),
    pltpu.VMEM((2, 3, 32, 128), F32),
    pltpu.VMEM((2, 3, 16, 256), F32),
]
GATE_SCRATCH = [pltpu.VMEM((6 * NCH, 8, 128), F32), pltpu.VMEM((128, 128), F32)]
PARAMS = pltpu.CompilerParams(vmem_limit_bytes=60 * 2**20)


def shards(states, active, fibre_index, fibre_angle, conduct, gate_half, gate_slope, gate_tau, conductance, reversal,
           block_elem, block_weight, node_disp, elem_node, elem_fibre, material):
    sizes = tuple(lax.axis_size(a) for a in ALL)
    pos = jnp.stack([lax.axis_index(a) for a in ALL]).astype(jnp.int32)
    gates = (gate_half, gate_slope, gate_tau, conductance, reversal)
    full = sds(NSTATE, CX, CY, CZ)
    s1, *faces, code_col, code_row = call(
        functools.partial(first_kernel, sizes),
        "first",
        (pos, active.reshape(2), fibre_index.reshape(2), *gates),
        (fibre_angle, conduct, block_elem.transpose(0, 2, 1), states),
        [full, *FACES, sds(256, 128), sds(8, 256)],
        GATE_SCRATCH,
    )
    halo, got1 = exchange(*faces)
    corner, passive, active_force = call(
        element_kernel,
        "elements",
        (material,),
        (fibre_angle, node_disp, elem_node, elem_fibre.reshape(1, ELEMS)),
        [sds(64, ELEMS), sds(8, NODES), sds(64, ELEMS)],
    )
    s2, *faces = call(
        functools.partial(second_kernel, sizes),
        "second",
        (pos, *gates),
        (s1, *halo, got1, corner, code_row, block_weight.transpose(0, 2, 1)),
        [full, *FACES],
        GATE_SCRATCH + STEP_SCRATCH + [pltpu.VMEM((16, 16, 128), F32)],
    )
    halo, got2 = exchange(*faces)
    plane = whole((1, CX, CY, CZ))
    blend = jnp.asarray(blend_table())
    rest = (*halo, got1, got2, code_col, elem_node, passive, active_force, blend)
    outs = [full, sds(3, CX, CY, CZ), sds(3, NODES)]
    return pl.pallas_call(
        functools.partial(third_kernel, sizes),
        grid=(1,),
        out_shape=outs,
        in_specs=[whole((3,), pltpu.SMEM), plane, *[whole(x.shape) for x in rest]],
        out_specs=[plane, whole(outs[1].shape), whole(outs[2].shape)],
        scratch_shapes=STEP_SCRATCH,
        input_output_aliases={1: 0},
        compiler_params=PARAMS,
        name="third",
    )(pos, s2, *rest)


def solution(mesh):
    in_specs = (
        P(None, "gx", "gy", "gz"),
        *[P("gx", "gy", "gz")] * 2,
        *[P()] * 7,
        *[P("gx", "gy", "gz")] * 2,
        *[P(None, ALL)] * 2,
        P(ALL),
        P(),
    )
    out_specs = (P(None, "gx", "gy", "gz"), P(None, "gx", "gy", "gz"), P(None, ALL))
    return jax.shard_map(shards, mesh=mesh, in_specs=in_specs, out_specs=out_specs, check_vma=False)
```

```python
import functools

import jax
import jax.numpy as jnp
import numpy as np
from jax import lax
from jax.experimental import pallas as pl
from jax.experimental.pallas import tpu as pltpu
from jax.sharding import PartitionSpec as P

NSTATE, NCH, NF = 19, 17, 64
CX, CY, CZ = 16, 16, 128
ELEMS, SLOTS, NODES = 256, 256, 512
ALL = ("gx", "gy", "gz")
HIGHEST = lax.Precision.HIGHEST
F32, BF16 = jnp.float32, jnp.bfloat16
NT = (((1,), (1,)), ((), ()))
TN = (((0,), (0,)), ((), ()))
CORNERS = [(q // 4, q // 2 % 2, q % 2) for q in range(8)]
HEAD = 2


def iota(shape, dim):
    return lax.broadcasted_iota(jnp.int32, shape, dim)


def neighbour(pos_ref, sizes, step):
    at = [pos_ref[d] + step[d] for d in range(3)]
    ok = (at[0] >= 0) & (at[0] < sizes[0])
    for d in (1, 2):
        ok = ok & (at[d] >= 0) & (at[d] < sizes[d])
    row = (at[0] * sizes[1] + at[1]) * sizes[2] + at[2]
    return jnp.where(ok, row, 0), ok


ROWS = 5
FIRST = pl.ds(0, 256, stride=ROWS)


def put_row(msg, peer, ok, values, place=1):
    row = ROWS * peer + place
    base = pl.ds(pl.multiple_of(row // 8 * 8, 8), 8)
    here = iota((8, 128), 0) == jnp.where(ok, row % 8, -1)
    pltpu.store(msg.at[base, :], jnp.broadcast_to(values, (8, 128)), mask=here)


def take_row(got, peer, ok, place, rows_each=ROWS):
    row = rows_each * peer + place
    rows = got[pl.ds(pl.multiple_of(row // 8 * 8, 8), 8), :]
    here = iota((8, 128), 0) == jnp.where(ok, row % 8, -1)
    return jnp.sum(jnp.where(here, rows, 0.0), axis=0, keepdims=True)


def parts3(x):
    first = x.astype(BF16)
    rest = x - first.astype(F32)
    second = rest.astype(BF16)
    third = (rest - second.astype(F32)).astype(BF16)
    return first, second, third


def frame_of(angles):
    a, b = angles[0:1, :], angles[1:2, :]
    return jnp.cos(a) * jnp.cos(b), jnp.sin(a) * jnp.cos(b), jnp.sin(b)


def gate_constants(half_ref, slope_ref, tau_ref, cond_ref, rev_ref, const):
    for c in range(NCH):
        scale = 0.5 / jnp.full((8, 128), slope_ref[c], F32)
        keep = jnp.exp(-1.0 / jnp.full((8, 128), tau_ref[c], F32))
        cond = jnp.full((8, 128), cond_ref[c], F32)
        const[c] = scale
        const[NCH + c] = -half_ref[c] * scale
        const[2 * NCH + c] = keep
        const[3 * NCH + c] = 0.5 * (1.0 - keep)
        const[4 * NCH + c] = cond
        const[5 * NCH + c] = cond * rev_ref[c]


GROUPS = ((0, 1), (1, 5), (5, 9), (9, 13), (13, 17), (17, NSTATE))


def fetches(hbm, vmem, sems):
    copies = []
    for n, (low, high) in enumerate(GROUPS):
        copies.append(pltpu.make_async_copy(hbm.at[low:high], vmem.at[low:high], sems.at[n]))
        copies[n].start()
    return copies


def drain(vmem, hbm, sems, n):
    low, high = GROUPS[n]
    copy = pltpu.make_async_copy(vmem.at[low:high], hbm.at[low:high], sems.at[n])
    copy.start()
    return copy


def twice(x):
    return jnp.concatenate([x, x], 0)


def ionic_step(volt, source, target, alive, const, total, moment, coming, hbm, left):
    leaving = []
    for n, (low, high) in enumerate(GROUPS):
        if coming[n] is not None:
            coming[n].wait()
        for s in range(max(low, 1), high):
            c = s - 1
            for half in range(2):

                @pl.loop(8 * half, 8 * half + 8, unroll=8)
                def _(x):
                    old = source[s, x]
                    if s < NSTATE - 1:
                        rise = jnp.tanh(volt[x] * twice(const[c]) + twice(const[NCH + c]))
                        lift = twice(const[3 * NCH + c])
                        new = old * twice(const[2 * NCH + c]) + (lift * rise + lift)
                        flow, shift_ = new * twice(const[4 * NCH + c]), new * twice(const[5 * NCH + c])
                        total[x] = flow if c == 0 else total[x] + flow
                        moment[x] = shift_ if c == 0 else moment[x] + shift_
                    else:
                        new = old * 0.9 + 0.1 * (0.5 * jnp.tanh(4.0 * (volt[x] - 0.5)) + 0.5)
                    target[s, x] = jnp.where(alive[half], new, old)

        if n:
            leaving.append(drain(target, hbm, left, n))
    for half in range(2):

        @pl.loop(8 * half, 8 * half + 8, unroll=8)
        def _(x):
            v = volt[x]
            target[0, x] = jnp.where(alive[half], v - (v * total[x] - moment[x]), v)

    return [*leaving, drain(target, hbm, left, 0)]


def send_faces(v, pos_ref, sizes, xlo, xhi, ylo, yhi, msg, lines):
    xlo[...] = v[0:2]
    xhi[...] = v[14:16]
    ylo[...] = v[:, 0:8, :]
    yhi[...] = v[:, 8:16, :]
    row, lane = iota((8, 128), 0), iota((8, 128), 1)
    pick = ((row < 4) & (lane == jnp.where(row < 2, row, row + 124))).astype(F32)
    flat = v[...].reshape(CX * CY, CZ)
    ends = lax.dot_general(pick, flat, NT, precision=HIGHEST, preferred_element_type=F32)
    for dz in (-1, 1):
        peer, ok = neighbour(pos_ref, sizes, (0, 0, dz))
        for n in range(4):
            k, half = n // 2 + (2 if dz > 0 else 0), n % 2
            put_row(msg, peer, ok, ends[k : k + 1, 128 * half : 128 * half + 128], 1 + n)
    lines[0:16] = v[0]
    lines[16:32] = v[15]
    for x in range(CX):
        lines[32 + x : 33 + x] = v[x, 0:1, :]
        lines[48 + x : 49 + x] = v[x, 15:16, :]
    lines[64:128] = jnp.zeros((64, 128), F32)
    marks = lax.dot_general(pick, lines[...], NT, precision=HIGHEST, preferred_element_type=F32)
    for dx in (-1, 1):
        for dy in (-1, 1):
            peer, ok = neighbour(pos_ref, sizes, (dx, dy, 0))
            edge = v[15 if dx > 0 else 0, (15 if dy > 0 else 0) : (16 if dy > 0 else 1), :]

            put_row(msg, peer, ok, edge)

    for step in ((-1, 0), (1, 0), (0, -1), (0, 1)):
        for dz in (-1, 1):
            peer, ok = neighbour(pos_ref, sizes, (*step, dz))
            edge = marks[3:4] if dz > 0 else marks[0:1]

            put_row(msg, peer, ok, edge)


def heads(pos_ref, sizes, got, step):
    row, ok = neighbour(pos_ref, sizes, step)
    return take_row(got, row, ok, 0, 1)


def entry(head, tile, which):
    lane = HEAD + 7 * tile + which
    return head[:, lane : lane + 1]


def edges_of(pos_ref, sizes, got, step):
    row, ok = neighbour(pos_ref, sizes, step)
    return take_row(got, row, ok, 1)


def tile_planes(pos_ref, sizes, got1, cx, cy, cz):
    own = heads(pos_ref, sizes, got1, (0, 0, 0))
    ends = {s: heads(pos_ref, sizes, got1, s) for s in ((-1, 0, 0), (1, 0, 0), (0, -1, 0), (0, 1, 0), (0, 0, -1), (0, 0, 1))}
    for k, (head, tile) in enumerate(((ends[-1, 0, 0], 1), (own, 0), (own, 1), (ends[1, 0, 0], 0))):
        for n, which in enumerate((0, 3, 4)):
            cx[k, n] = jnp.broadcast_to(entry(head, tile, which), (16, 128))
    rows, lanes = iota((32, 128), 0), iota((16, 256), 1)
    for tile in range(2):
        for n, which in enumerate((3, 1, 5)):
            cy[tile, n] = jnp.where(
                rows == 7,
                entry(ends[0, -1, 0], tile, which),
                jnp.where(rows == 24, entry(ends[0, 1, 0], tile, which), entry(own, tile, which)),
            )
        for n, which in enumerate((4, 5, 2)):
            cz[tile, n] = jnp.where(
                lanes == 255,
                entry(ends[0, 0, -1], tile, which),
                jnp.where(lanes == 128, entry(ends[0, 0, 1], tile, which), entry(own, tile, which)),
            )
    return entry(own, 0, 6), entry(own, 1, 6)


def fill_extended(vext, v, faces, got, pos_ref, sizes):
    xm, xp, ym, yp = faces
    vext[2:18, 8:24, 0:128] = v[...]
    vext[0:2, 8:24, 0:128] = xm[...]
    vext[18:20, 8:24, 0:128] = xp[...]
    vext[2:18, 0:8, 0:128] = ym[...]
    vext[2:18, 24:32, 0:128] = yp[...]
    row, lane = iota((8, 128), 0), iota((8, 128), 1)
    place = ((row < 4) & (lane == jnp.where(row < 2, row + 126, row - 2))).astype(F32)
    outer = []
    for dz in (-1, 1):
        peer, ok = neighbour(pos_ref, sizes, (0, 0, dz))
        for k in range(2):
            outer.append(jnp.concatenate([take_row(got, peer, ok, 1 + 2 * k + half) for half in range(2)], 1))
    outer = jnp.concatenate([*outer, jnp.zeros((4, 256), F32)], 0)
    beyond = lax.dot_general(outer, place, TN, precision=HIGHEST, preferred_element_type=F32)
    vext[2:18, 8:24, 128:256] = beyond.reshape(16, 16, 128)
    for dx, i in ((-1, 1), (1, 18)):
        for dy, j in ((-1, 7), (1, 24)):
            vext[i, j : j + 1, 0:128] = edges_of(pos_ref, sizes, got, (dx, dy, 0))
    lanes = iota((1, 128), 1)
    group = lanes // 16
    lines = []
    for dz in (-1, 1):
        line = jnp.zeros((1, 128), F32)
        for g, (dx, dy) in enumerate(((1, 0), (-1, 0), (0, 1), (0, -1))):
            line = jnp.where(group == g, edges_of(pos_ref, sizes, got, (dx, dy, dz)), line)
        lines.append(line)
    outer = jnp.concatenate([*lines, jnp.zeros((6, 128), F32)], 0)
    place = ((row < 2) & (lane == jnp.where(row == 0, 127, 0))).astype(F32)
    beyond = lax.dot_general(outer, place, TN, precision=HIGHEST, preferred_element_type=F32)
    vext[18, 8:24, 128:256] = beyond[0:16]
    vext[1, 8:24, 128:256] = beyond[16:32]
    for x in range(CX):
        vext[2 + x, 24:25, 128:256] = beyond[32 + x : 33 + x]
        vext[2 + x, 7:8, 128:256] = beyond[48 + x : 49 + x]


def flux_x(vext, fx, cx):
    def one(p, tile):
        wide = vext[p, 8:24, :]
        gx = vext[p + 1, 8:24, 0:128] - vext[p - 1, 8:24, 0:128]
        gy = vext[p, 9:25, 0:128] - vext[p, 7:23, 0:128]
        gz = (pltpu.roll(wide, 255, 1) - pltpu.roll(wide, 1, 1))[:, 0:128]
        fx[p - 1] = cx[tile, 0] * gx + cx[tile, 1] * gy + cx[tile, 2] * gz

    one(1, 0)
    one(18, 3)

    @pl.loop(2, 18, unroll=4)
    def _(p):
        one(p, jnp.where(p < 10, 1, 2))


def lap_plane(vext, fx, cy, cz, x):
    p = x + 2
    tile = x // 8
    wide = vext[p]
    gx = vext[p + 1] - vext[p - 1]
    gy = pltpu.roll(wide, 31, 0) - pltpu.roll(wide, 1, 0)
    gz = pltpu.roll(wide, 255, 1) - pltpu.roll(wide, 1, 1)
    fy = cy[tile, 0] * gx[:, 0:128] + cy[tile, 1] * gy[:, 0:128] + cy[tile, 2] * gz[:, 0:128]
    dy = (pltpu.roll(fy, 31, 0) - pltpu.roll(fy, 1, 0))[8:24]
    fz = cz[tile, 0] * gx[8:24] + cz[tile, 1] * gy[8:24] + cz[tile, 2] * gz[8:24]
    dz = (pltpu.roll(fz, 255, 1) - pltpu.roll(fz, 1, 1))[:, 0:128]
    return 0.25 * (fx[x + 2] - fx[x] + dy + dz)


def blocks(ref):
    return jnp.concatenate([ref[n].T for n in range(8)], 0)


def column_wide(values):
    return jnp.concatenate([jnp.broadcast_to(values[:, z : z + 1], (64, 256)) for z in range(4)], 0)


def to_row(wide):
    return jnp.sum(jnp.where(iota((256, 256), 0) == iota((256, 256), 1), wide, 0.0), axis=0, keepdims=True)


def first_kernel(sizes, pos_ref, act_ref, fi_ref, half_ref, slope_ref, tau_ref, cond_ref, rev_ref, angle, conduct, block_elem,
                 states_hbm, s1_hbm, xlo, xhi, ylo, yhi, msg, code_col, code_row, const, lines, states, s1, came, left, total, moment):
    coming = fetches(states_hbm, states, came)
    gate_constants(half_ref, slope_ref, tau_ref, cond_ref, rev_ref, const)
    ids = blocks(block_elem)
    owner = column_wide((ids // ELEMS).astype(F32))
    local = column_wide((ids % ELEMS).astype(F32))
    owner_row = to_row(owner)
    before = iota((256, 256), 1) < iota((256, 256), 0)
    rank = jnp.sum(jnp.where((owner == owner_row) & before, 1.0, 0.0), axis=1, keepdims=True)
    code = owner + 256.0 * rank
    code_col[...] = code[:, 0:128]
    row_code = to_row(code)
    code_row[...] = jnp.broadcast_to(row_code, (8, 256))
    local_row = to_row(local) + 1.0
    peers = iota((256, 256), 0).astype(F32)
    lane = iota((1, 128), 1)
    a, b = frame_of(angle), conduct[...]
    spread = b[0:1] - b[1:2]
    entries = [b[1:2] + spread * a[n] * a[n] for n in range(3)]
    entries += [spread * a[0] * a[1], spread * a[0] * a[2], spread * a[1] * a[2]]
    head = jnp.zeros((1, 128), F32)
    slots = iota((1, NF), 1)
    for tile in range(2):
        alive = (act_ref[tile] > 0).astype(F32)
        chosen = slots == fi_ref[tile]
        for n in range(6):
            value = jnp.sum(jnp.where(chosen, entries[n], 0.0), axis=1, keepdims=True) * alive
            head = jnp.where(lane == HEAD + 7 * tile + n, value, head)
        head = jnp.where(lane == HEAD + 7 * tile + 6, alive, head)
    asked = jnp.broadcast_to(head, (256, 128))
    target = iota((128, 256), 0)
    for r in range(2):
        goes = (row_code == peers + 256.0 * r).astype(F32).astype(BF16)
        labels = jnp.where(target == r, local_row, 0.0).astype(BF16)
        asked += lax.dot_general(goes, labels, NT, preferred_element_type=F32)
    msg[...] = jnp.zeros((ROWS * 256, 128), F32)
    msg[FIRST, :] = asked
    alive = [act_ref[half] > 0 for half in range(2)]
    leaving = ionic_step(states.at[0], states, s1, alive, const, total, moment, coming, s1_hbm, left)
    send_faces(s1.at[0], pos_ref, sizes, xlo, xhi, ylo, yhi, msg, lines)
    for copy in leaving:
        copy.wait()


def element_kernel(material, angle, node_disp, elem_node, elem_fibre, corner, passive, active):
    table = jnp.concatenate([*frame_of(angle), jnp.zeros((5, NF), F32)], 0)
    hot = (iota((NF, ELEMS), 0) == elem_fibre[...]).astype(F32)
    fibre = jnp.dot(table, hot, precision=HIGHEST, preferred_element_type=F32)
    f = [fibre[j : j + 1] for j in range(3)]
    disp = jnp.concatenate([node_disp[...], jnp.zeros((5, NODES), F32)], 0)
    packed = jnp.concatenate([p.astype(F32) for p in parts3(disp)] + [jnp.zeros((8, NODES), F32)], 0).astype(BF16)
    slope = [jnp.zeros((8, ELEMS), F32) for _ in range(3)]
    for q in range(8):
        hot = (iota((NODES, ELEMS), 0) == elem_node[q : q + 1, :]).astype(F32).astype(BF16)
        got = jnp.dot(packed, hot, preferred_element_type=F32)
        got = got[0:8] + got[8:16] + got[16:24]
        corner[8 * q : 8 * q + 8] = got
        for j in range(3):
            slope[j] += got if CORNERS[q][j] else -got
    F = [[slope[j][i : i + 1] * 0.25 + (1.0 if i == j else 0.0) for j in range(3)] for i in range(3)]

    def cofactor(i, j):
        a, b = [n for n in range(3) if n != i]
        c, d = [n for n in range(3) if n != j]
        minor = F[a][c] * F[b][d] - F[a][d] * F[b][c]
        return minor if (i + j) % 2 == 0 else -minor

    cof = [[cofactor(i, j) for j in range(3)] for i in range(3)]
    volume = F[0][0] * cof[0][0] + F[0][1] * cof[0][1] + F[0][2] * cof[0][2]
    invert = 1.0 / volume
    bulk = material[1] * jnp.log(volume)
    none = jnp.zeros((5, ELEMS), F32)
    stress, fibres = [], []
    stretch = [F[i][0] * f[0] + F[i][1] * f[1] + F[i][2] * f[2] for i in range(3)]
    for j in range(3):
        rows = []
        for i in range(3):
            inverse = cof[i][j] * invert
            rows.append(material[0] * (F[i][j] - inverse) + bulk * inverse)
        stress.append(jnp.concatenate([*rows, none], 0))
        fibres.append(jnp.concatenate([*[material[2] * stretch[i] * f[j] for i in range(3)], none], 0))
    total = jnp.zeros((24, NODES), F32)
    for q in range(8):
        sign = [0.25 if CORNERS[q][j] else -0.25 for j in range(3)]
        force = stress[0] * sign[0] + stress[1] * sign[1] + stress[2] * sign[2]
        active[8 * q : 8 * q + 8] = fibres[0] * sign[0] + fibres[1] * sign[1] + fibres[2] * sign[2]
        hot = (iota((NODES, ELEMS), 0) == elem_node[q : q + 1, :]).astype(F32).astype(BF16)
        packed = jnp.concatenate([p.astype(F32) for p in parts3(force)], 0).astype(BF16)
        total += lax.dot_general(packed, hot, NT, preferred_element_type=F32)
    passive[...] = total[0:8] + total[8:16] + total[16:24]


def second_kernel(sizes, pos_ref, half_ref, slope_ref, tau_ref, cond_ref, rev_ref, s1_hbm, xm, xp, ym, yp, got1, corner,
                  code_row, block_weight, s2_hbm, xlo, xhi, ylo, yhi, msg, heard, const, lines, s1, s2, came, left, total, moment, vext, fx, cx, cy, cz,
                  tens):
    coming = fetches(s1_hbm, s1, came)
    gate_constants(half_ref, slope_ref, tau_ref, cond_ref, rev_ref, const)
    heard[...] = got1[FIRST, :]
    live = tile_planes(pos_ref, sizes, heard, cx, cy, cz)
    coming[0].wait()
    fill_extended(vext, s1.at[0], (xm, xp, ym, yp), got1, pos_ref, sizes)
    flux_x(vext, fx, cx)

    @pl.loop(0, CX, unroll=4)
    def _(x):
        here = jnp.where(x < 8, live[0], live[1])
        tens[x] = s1[0, x] + here * lap_plane(vext, fx, cy, cz, x)

    alive = [jnp.broadcast_to(here, (16, 128)) > 0.5 for here in live]
    leaving = ionic_step(tens, s1, s2, alive, const, total, moment, [None, *coming[1:]], s2_hbm, left)
    for n in range(8):
        ratio = jnp.zeros((16, 128), F32)
        for x in (2 * n, 2 * n + 1):
            square = s2[NSTATE - 1, x] * s2[NSTATE - 1, x]
            ratio += square / (square + 0.09)
        lines[16 * n : 16 * n + 16] = ratio
    pairs = lines[...]
    row, lane = iota((64, 128), 0), iota((64, 128), 1)
    over_y = ((row // 8 == lane // 16) & (row % 8 == lane % 16 // 2)).astype(F32)
    over_z = jnp.where(iota((128, 128), 0) // 32 == iota((128, 128), 1), 1.0 / 128.0, 0.0)
    mean = jnp.dot(over_y, pairs, precision=HIGHEST, preferred_element_type=F32)
    mean = jnp.dot(mean, over_z, precision=HIGHEST, preferred_element_type=F32)
    value = to_row(column_wide(mean[:, 0:4] * blocks(block_weight)))
    peers = iota((256, 256), 0).astype(F32)
    elems = iota((256, 256), 1).astype(F32)
    target = iota((128, 256), 0)
    answer = jnp.zeros((256, 128), F32)
    asked = heard[...]
    none = jnp.zeros((64, 256), F32)
    for r in range(2):
        goes = (code_row[0:1, :] == peers + 256.0 * r).astype(F32).astype(BF16)
        for part in parts3(jnp.where(target == 64 * r + 3, value, 0.0)):
            answer += lax.dot_general(goes, part, NT, preferred_element_type=F32)
        wants = (asked[:, r : r + 1] == elems + 1.0).astype(F32).astype(BF16)
        held = jnp.concatenate([corner[...], none] if r == 0 else [none, corner[...]], 0)
        for part in parts3(held)[:2]:
            answer += lax.dot_general(wants, part, NT, preferred_element_type=F32)
    msg[...] = jnp.zeros((ROWS * 256, 128), F32)
    msg[FIRST, :] = answer
    send_faces(s2.at[0], pos_ref, sizes, xlo, xhi, ylo, yhi, msg, lines)
    for copy in leaving:
        copy.wait()


def third_kernel(sizes, pos_ref, s2, xm, xp, ym, yp, heard, got2, code_col, elem_node, passive, active, blend_hbm, s3, fine,
                 residual, vext, fx, cx, cy, cz, blend, came):
    coming = pltpu.make_async_copy(blend_hbm, blend, came)
    coming.start()
    live = tile_planes(pos_ref, sizes, heard, cx, cy, cz)
    fill_extended(vext, s2.at[0], (xm, xp, ym, yp), got2, pos_ref, sizes)
    flux_x(vext, fx, cx)

    @pl.loop(0, CX, unroll=4)
    def _(x):
        here = jnp.where(x < 8, live[0], live[1])
        s3[0, x] = s2[0, x] + here * lap_plane(vext, fx, cy, cz, x)

    elems = iota((256, 256), 1).astype(F32)
    tension = jnp.zeros((1, 256), F32)
    asked, answer = heard[...], got2[FIRST, :]
    for r in range(2):
        wants = asked[:, r : r + 1] == elems + 1.0
        tension += jnp.sum(jnp.where(wants, answer[:, 64 * r + 3 : 64 * r + 4], 0.0), axis=0, keepdims=True)
    total = jnp.zeros((24, NODES), F32)
    for q in range(8):
        hot = (iota((NODES, ELEMS), 0) == elem_node[q : q + 1, :]).astype(F32).astype(BF16)
        packed = jnp.concatenate([p.astype(F32) for p in parts3(active[8 * q : 8 * q + 8] * tension)], 0).astype(BF16)
        total += lax.dot_general(packed, hot, NT, preferred_element_type=F32)
    total = passive[...] + total[0:8] + total[8:16] + total[16:24]
    residual[...] = total[0:3]

    code = jnp.concatenate([code_col[...], code_col[...]], 1)
    lane = iota((256, 128), 1)
    disp = jnp.zeros((256, 128), F32)
    for r in range(2):
        goes = (code == elems + 256.0 * r).astype(F32).astype(BF16)
        part = jnp.where(lane // 64 == r, answer, 0.0)
        part = part if r == 0 else pltpu.roll(part, 64, 1)
        for piece in parts3(part)[:2]:
            disp += jnp.dot(goes, piece, preferred_element_type=F32)
    merged = jnp.concatenate(
        [disp[0:64] + pltpu.roll(disp[64:128], 64, 1), disp[128:192] + pltpu.roll(disp[192:256], 64, 1)], 1
    )
    which = iota((64, 256), 1) % 8
    rows = jnp.concatenate([jnp.where(which == c, merged, 0.0) for c in range(3)], 0)
    first, second, _ = parts3(rows)
    coming.wait()
    out = jnp.dot(first, blend[0], preferred_element_type=F32) + jnp.dot(second, blend[0], preferred_element_type=F32)
    out += jnp.dot(first, blend[1], preferred_element_type=F32)
    for c in range(3):
        for bx in range(8):
            tile = out[64 * c + 8 * bx : 64 * c + 8 * bx + 8]
            for i in range(2):
                for j in range(2):
                    at = 128 * (2 * i + j)
                    fine[c, 2 * bx + i, pl.ds(j, 8, stride=2), :] = tile[:, at : at + 128]


def blend_table():
    table = np.zeros((4, 8, 8, 2, 2, 128), np.float64)
    z = np.arange(128)
    for q, bits in enumerate(CORNERS):
        for i in range(2):
            for j in range(2):
                for bz in range(4):
                    xi = ((i + 0.5) / 2, (j + 0.5) / 2, (z % 32 + 0.5) / 32)
                    w = 1.0
                    for d in range(3):
                        w = w * (xi[d] if bits[d] else 1.0 - xi[d])
                    table[bz, q, :, i, j] = w * (z // 32 == bz)
    table = table.reshape(256, 512)
    import ml_dtypes

    first = table.astype(ml_dtypes.bfloat16)
    second = (table - first.astype(np.float64)).astype(ml_dtypes.bfloat16)
    return np.stack([first, second])


def shift(x, axis, by):
    count = lax.axis_size(axis)
    pairs = [(i, i + by) for i in range(count) if 0 <= i + by < count]
    return lax.ppermute(x, axis, pairs)


def exchange(xlo, xhi, ylo, yhi, msg):
    got = lax.all_to_all(msg.reshape(256, 1, ROWS * 128), ALL, 0, 0, tiled=True).reshape(ROWS * 256, 128)
    halo = shift(xhi, "gx", 1), shift(xlo, "gx", -1), shift(yhi, "gy", 1), shift(ylo, "gy", -1)
    return halo, got


def whole(shape, space=None):
    return pl.BlockSpec(shape, lambda i: (0,) * len(shape), memory_space=space)


ANYWHERE = pl.BlockSpec(memory_space=pl.ANY)


def call(body, name, scalars, arrays, outs, scratch=(), far=(), mebibytes=50):
    specs = [ANYWHERE if n in far else whole(x.shape) for n, x in enumerate([*arrays, *outs])]
    return pl.pallas_call(
        body,
        grid=(1,),
        out_shape=outs,
        in_specs=[whole(x.shape, pltpu.SMEM) for x in scalars] + specs[: len(arrays)],
        out_specs=specs[len(arrays) :],
        scratch_shapes=scratch,
        compiler_params=grant(mebibytes),
        name=name,
    )(*scalars, *arrays)


def sds(*shape):
    return jax.ShapeDtypeStruct(shape, F32)


FACES = [sds(2, 16, 128), sds(2, 16, 128), sds(16, 8, 128), sds(16, 8, 128), sds(ROWS * 256, 128)]
STEP_SCRATCH = [
    pltpu.VMEM((20, 32, 256), F32),
    pltpu.VMEM((18, 16, 128), F32),
    pltpu.VMEM((4, 3, 16, 128), F32),
    pltpu.VMEM((2, 3, 32, 128), F32),
    pltpu.VMEM((2, 3, 16, 256), F32),
]
STATE_SCRATCH = [
    pltpu.VMEM((NSTATE, CX, CY, CZ), F32),
    pltpu.VMEM((NSTATE, CX, CY, CZ), F32),
    pltpu.SemaphoreType.DMA((len(GROUPS),)),
    pltpu.SemaphoreType.DMA((len(GROUPS),)),
    pltpu.VMEM((CX, CY, CZ), F32),
    pltpu.VMEM((CX, CY, CZ), F32),
]
GATE_SCRATCH = [pltpu.VMEM((6 * NCH, 8, 128), F32), pltpu.VMEM((128, 128), F32)]
def grant(mebibytes):
    return pltpu.CompilerParams(vmem_limit_bytes=mebibytes * 2**20)


def shards(states, active, fibre_index, fibre_angle, conduct, gate_half, gate_slope, gate_tau, conductance, reversal,
           block_elem, block_weight, node_disp, elem_node, elem_fibre, material):
    sizes = tuple(lax.axis_size(a) for a in ALL)
    pos = jnp.stack([lax.axis_index(a) for a in ALL]).astype(jnp.int32)
    gates = (gate_half, gate_slope, gate_tau, conductance, reversal)
    full = sds(NSTATE, CX, CY, CZ)
    s1, *faces, code_col, code_row = call(
        functools.partial(first_kernel, sizes),
        "first",
        (pos, active.reshape(2), fibre_index.reshape(2), *gates),
        (fibre_angle, conduct, block_elem.transpose(0, 2, 1), states),
        [full, *FACES, sds(256, 128), sds(8, 256)],
        GATE_SCRATCH + STATE_SCRATCH,
        (3, 4),
        60,
    )
    halo, got1 = exchange(*faces)
    corner, passive, active_force = call(
        element_kernel,
        "elements",
        (material,),
        (fibre_angle, node_disp, elem_node, elem_fibre.reshape(1, ELEMS)),
        [sds(64, ELEMS), sds(8, NODES), sds(64, ELEMS)],
    )
    s2, *faces, heard = call(
        functools.partial(second_kernel, sizes),
        "second",
        (pos, *gates),
        (s1, *halo, got1, corner, code_row, block_weight.transpose(0, 2, 1)),
        [full, *FACES, sds(256, 128)],
        GATE_SCRATCH + STATE_SCRATCH + STEP_SCRATCH + [pltpu.VMEM((16, 16, 128), F32)],
        (0, 9),
    )
    halo, got2 = exchange(*faces)
    plane = whole((1, CX, CY, CZ))
    blend = jnp.asarray(blend_table())
    rest = (*halo, heard, got2, code_col, elem_node, passive, active_force)
    outs = [full, sds(3, CX, CY, CZ), sds(3, NODES)]
    return pl.pallas_call(
        functools.partial(third_kernel, sizes),
        grid=(1,),
        out_shape=outs,
        in_specs=[whole((3,), pltpu.SMEM), plane, *[whole(x.shape) for x in rest], ANYWHERE],
        out_specs=[plane, whole(outs[1].shape), whole(outs[2].shape)],
        scratch_shapes=STEP_SCRATCH + [pltpu.VMEM(blend.shape, BF16), pltpu.SemaphoreType.DMA],
        input_output_aliases={1: 0},
        compiler_params=grant(50),
        name="third",
    )(pos, s2, *rest, blend)


def solution(mesh):
    in_specs = (
        P(None, "gx", "gy", "gz"),
        *[P("gx", "gy", "gz")] * 2,
        *[P()] * 7,
        *[P("gx", "gy", "gz")] * 2,
        *[P(None, ALL)] * 2,
        P(ALL),
        P(),
    )
    out_specs = (P(None, "gx", "gy", "gz"), P(None, "gx", "gy", "gz"), P(None, ALL))
    return jax.shard_map(shards, mesh=mesh, in_specs=in_specs, out_specs=out_specs, check_vma=False)
```

```python
import functools

import jax
import jax.numpy as jnp
import numpy as np
from jax import lax
from jax.experimental import pallas as pl
from jax.experimental.pallas import tpu as pltpu
from jax.sharding import PartitionSpec as P

NSTATE, NCH, NF = 19, 17, 64
CX, CY, CZ = 16, 16, 128
ELEMS, SLOTS, NODES = 256, 256, 512
ALL = ("gx", "gy", "gz")
HIGHEST = lax.Precision.HIGHEST
F32, BF16 = jnp.float32, jnp.bfloat16
NT = (((1,), (1,)), ((), ()))
TN = (((0,), (0,)), ((), ()))
CORNERS = [(q // 4, q // 2 % 2, q % 2) for q in range(8)]
HEAD = 2


def iota(shape, dim):
    return lax.broadcasted_iota(jnp.int32, shape, dim)


def place():
    return [lax.axis_index(a) for a in ALL]


def neighbour(pos_ref, sizes, step):
    at = [pos_ref[d] + step[d] for d in range(3)]
    ok = (at[0] >= 0) & (at[0] < sizes[0])
    for d in (1, 2):
        ok = ok & (at[d] >= 0) & (at[d] < sizes[d])
    row = (at[0] * sizes[1] + at[1]) * sizes[2] + at[2]
    return jnp.where(ok, row, 0), ok


ROWS = 5
FIRST = pl.ds(0, 256, stride=ROWS)


def put_row(msg, peer, ok, values, place=1):
    row = ROWS * peer + place
    base = pl.ds(pl.multiple_of(row // 8 * 8, 8), 8)
    here = iota((8, 128), 0) == jnp.where(ok, row % 8, -1)
    pltpu.store(msg.at[base, :], jnp.broadcast_to(values, (8, 128)), mask=here)


def take_row(got, peer, ok, place, rows_each=ROWS):
    row = rows_each * peer + place
    rows = got[pl.ds(pl.multiple_of(row // 8 * 8, 8), 8), :]
    here = iota((8, 128), 0) == jnp.where(ok, row % 8, -1)
    return jnp.sum(jnp.where(here, rows, 0.0), axis=0, keepdims=True)


def parts3(x):
    first = x.astype(BF16)
    rest = x - first.astype(F32)
    second = rest.astype(BF16)
    third = (rest - second.astype(F32)).astype(BF16)
    return first, second, third


def frame_of(angles):
    a, b = angles[0:1, :], angles[1:2, :]
    return jnp.cos(a) * jnp.cos(b), jnp.sin(a) * jnp.cos(b), jnp.sin(b)


def gate_constants(half_ref, slope_ref, tau_ref, cond_ref, rev_ref, const):
    for c in range(NCH):
        scale = 0.5 / jnp.full((8, 128), slope_ref[c], F32)
        keep = jnp.exp(-1.0 / jnp.full((8, 128), tau_ref[c], F32))
        cond = jnp.full((8, 128), cond_ref[c], F32)
        const[c] = scale
        const[NCH + c] = -half_ref[c] * scale
        const[2 * NCH + c] = keep
        const[3 * NCH + c] = 0.5 * (1.0 - keep)
        const[4 * NCH + c] = cond
        const[5 * NCH + c] = cond * rev_ref[c]


GROUPS = ((0, 1), (1, 5), (5, 9), (9, 13), (13, 17), (17, NSTATE))


def fetches(hbm, vmem, sems):
    copies = []
    for n, (low, high) in enumerate(GROUPS):
        copies.append(pltpu.make_async_copy(hbm.at[low:high], vmem.at[low:high], sems.at[n]))
        copies[n].start()
    return copies


def drain(vmem, hbm, sems, n):
    low, high = GROUPS[n]
    copy = pltpu.make_async_copy(vmem.at[low:high], hbm.at[low:high], sems.at[n])
    copy.start()
    return copy


def twice(x):
    return jnp.concatenate([x, x], 0)


def ionic_step(volt, source, target, alive, const, total, moment, coming, hbm, left):
    leaving = []
    for n, (low, high) in enumerate(GROUPS):
        if coming[n] is not None:
            coming[n].wait()
        for s in range(max(low, 1), high):
            c = s - 1
            for half in range(2):

                @pl.loop(8 * half, 8 * half + 8, unroll=8)
                def _(x):
                    old = source[s, x]
                    if s < NSTATE - 1:
                        rise = jnp.tanh(volt[x] * twice(const[c]) + twice(const[NCH + c]))
                        lift = twice(const[3 * NCH + c])
                        new = old * twice(const[2 * NCH + c]) + (lift * rise + lift)
                        flow, shift_ = new * twice(const[4 * NCH + c]), new * twice(const[5 * NCH + c])
                        total[x] = flow if c == 0 else total[x] + flow
                        moment[x] = shift_ if c == 0 else moment[x] + shift_
                    else:
                        new = old * 0.9 + 0.1 * (0.5 * jnp.tanh(4.0 * (volt[x] - 0.5)) + 0.5)
                    target[s, x] = jnp.where(alive[half], new, old)

        if n:
            leaving.append(drain(target, hbm, left, n))
    for half in range(2):

        @pl.loop(8 * half, 8 * half + 8, unroll=8)
        def _(x):
            v = volt[x]
            target[0, x] = jnp.where(alive[half], v - (v * total[x] - moment[x]), v)

    return [*leaving, drain(target, hbm, left, 0)]


def send_faces(v, pos_ref, sizes, xlo, xhi, ylo, yhi, msg, lines):
    xlo[...] = v[0:2]
    xhi[...] = v[14:16]
    for x in range(CX):
        for n in range(2):
            ylo[n, x : x + 1] = v[x, n : n + 1, :]
            yhi[n, x : x + 1] = v[x, 14 + n : 15 + n, :]
    row, lane = iota((8, 128), 0), iota((8, 128), 1)
    pick = ((row < 4) & (lane == jnp.where(row < 2, row, row + 124))).astype(F32)
    flat = v[...].reshape(CX * CY, CZ)
    ends = lax.dot_general(pick, flat, NT, precision=HIGHEST, preferred_element_type=F32)
    for dz in (-1, 1):
        peer, ok = neighbour(pos_ref, sizes, (0, 0, dz))
        for n in range(4):
            k, half = n // 2 + (2 if dz > 0 else 0), n % 2
            put_row(msg, peer, ok, ends[k : k + 1, 128 * half : 128 * half + 128], 1 + n)
    lines[0:16] = v[0]
    lines[16:32] = v[15]
    lines[32:48] = ylo[0]
    lines[48:64] = yhi[1]
    lines[64:128] = jnp.zeros((64, 128), F32)
    marks = lax.dot_general(pick, lines[...], NT, precision=HIGHEST, preferred_element_type=F32)
    for dx in (-1, 1):
        for dy in (-1, 1):
            peer, ok = neighbour(pos_ref, sizes, (dx, dy, 0))
            edge = v[15 if dx > 0 else 0, (15 if dy > 0 else 0) : (16 if dy > 0 else 1), :]

            put_row(msg, peer, ok, edge)

    for step in ((-1, 0), (1, 0), (0, -1), (0, 1)):
        for dz in (-1, 1):
            peer, ok = neighbour(pos_ref, sizes, (*step, dz))
            edge = marks[3:4] if dz > 0 else marks[0:1]

            put_row(msg, peer, ok, edge)


def heads(pos_ref, sizes, got, step):
    row, ok = neighbour(pos_ref, sizes, step)
    return take_row(got, row, ok, 0, 1)


def entry(head, tile, which):
    lane = HEAD + 7 * tile + which
    return head[:, lane : lane + 1]


def edges_of(pos_ref, sizes, got, step):
    row, ok = neighbour(pos_ref, sizes, step)
    return take_row(got, row, ok, 1)


def tile_planes(pos_ref, sizes, got1, cx, cy, cz):
    own = heads(pos_ref, sizes, got1, (0, 0, 0))
    ends = {s: heads(pos_ref, sizes, got1, s) for s in ((-1, 0, 0), (1, 0, 0), (0, -1, 0), (0, 1, 0), (0, 0, -1), (0, 0, 1))}
    for k, (head, tile) in enumerate(((ends[-1, 0, 0], 1), (own, 0), (own, 1), (ends[1, 0, 0], 0))):
        for n, which in enumerate((0, 3, 4)):
            cx[k, n] = jnp.broadcast_to(entry(head, tile, which), (16, 128))
    rows, lanes = iota((32, 128), 0), iota((16, 256), 1)
    for tile in range(2):
        for n, which in enumerate((3, 1, 5)):
            cy[tile, n] = jnp.where(
                rows == 7,
                entry(ends[0, -1, 0], tile, which),
                jnp.where(rows == 24, entry(ends[0, 1, 0], tile, which), entry(own, tile, which)),
            )
        for n, which in enumerate((4, 5, 2)):
            cz[tile, n] = jnp.where(
                lanes == 255,
                entry(ends[0, 0, -1], tile, which),
                jnp.where(lanes == 128, entry(ends[0, 0, 1], tile, which), entry(own, tile, which)),
            )
    return entry(own, 0, 6), entry(own, 1, 6)


def fill_extended(vext, v, faces, got, pos_ref, sizes):
    xm, xp, ym, yp = faces
    vext[2:18, 8:24, 0:128] = v[...]
    vext[0:2, 8:24, 0:128] = xm[...]
    vext[18:20, 8:24, 0:128] = xp[...]
    for x in range(CX):
        for n in range(2):
            vext[2 + x, 6 + n : 7 + n, 0:128] = ym[n, x : x + 1]
            vext[2 + x, 24 + n : 25 + n, 0:128] = yp[n, x : x + 1]
    row, lane = iota((8, 128), 0), iota((8, 128), 1)
    place = ((row < 4) & (lane == jnp.where(row < 2, row + 126, row - 2))).astype(F32)
    outer = []
    for dz in (-1, 1):
        peer, ok = neighbour(pos_ref, sizes, (0, 0, dz))
        for k in range(2):
            outer.append(jnp.concatenate([take_row(got, peer, ok, 1 + 2 * k + half) for half in range(2)], 1))
    outer = jnp.concatenate([*outer, jnp.zeros((4, 256), F32)], 0)
    beyond = lax.dot_general(outer, place, TN, precision=HIGHEST, preferred_element_type=F32)
    vext[2:18, 8:24, 128:256] = beyond.reshape(16, 16, 128)
    for dx, i in ((-1, 1), (1, 18)):
        for dy, j in ((-1, 7), (1, 24)):
            vext[i, j : j + 1, 0:128] = edges_of(pos_ref, sizes, got, (dx, dy, 0))
    lanes = iota((1, 128), 1)
    group = lanes // 16
    lines = []
    for dz in (-1, 1):
        line = jnp.zeros((1, 128), F32)
        for g, (dx, dy) in enumerate(((1, 0), (-1, 0), (0, 1), (0, -1))):
            line = jnp.where(group == g, edges_of(pos_ref, sizes, got, (dx, dy, dz)), line)
        lines.append(line)
    outer = jnp.concatenate([*lines, jnp.zeros((6, 128), F32)], 0)
    place = ((row < 2) & (lane == jnp.where(row == 0, 127, 0))).astype(F32)
    beyond = lax.dot_general(outer, place, TN, precision=HIGHEST, preferred_element_type=F32)
    vext[18, 8:24, 128:256] = beyond[0:16]
    vext[1, 8:24, 128:256] = beyond[16:32]
    for x in range(CX):
        vext[2 + x, 24:25, 128:256] = beyond[32 + x : 33 + x]
        vext[2 + x, 7:8, 128:256] = beyond[48 + x : 49 + x]


def flux_x(vext, fx, cx):
    def one(p, tile):
        wide = vext[p, 8:24, :]
        gx = vext[p + 1, 8:24, 0:128] - vext[p - 1, 8:24, 0:128]
        gy = vext[p, 9:25, 0:128] - vext[p, 7:23, 0:128]
        gz = (pltpu.roll(wide, 255, 1) - pltpu.roll(wide, 1, 1))[:, 0:128]
        fx[p - 1] = cx[tile, 0] * gx + cx[tile, 1] * gy + cx[tile, 2] * gz

    one(1, 0)
    one(18, 3)

    @pl.loop(2, 18, unroll=4)
    def _(p):
        one(p, jnp.where(p < 10, 1, 2))


def lap_plane(vext, fx, cy, cz, x):
    p = x + 2
    tile = x // 8
    wide = vext[p]
    gx = vext[p + 1] - vext[p - 1]
    gy = pltpu.roll(wide, 31, 0) - pltpu.roll(wide, 1, 0)
    gz = pltpu.roll(wide, 255, 1) - pltpu.roll(wide, 1, 1)
    fy = cy[tile, 0] * gx[:, 0:128] + cy[tile, 1] * gy[:, 0:128] + cy[tile, 2] * gz[:, 0:128]
    dy = (pltpu.roll(fy, 31, 0) - pltpu.roll(fy, 1, 0))[8:24]
    fz = cz[tile, 0] * gx[8:24] + cz[tile, 1] * gy[8:24] + cz[tile, 2] * gz[8:24]
    dz = (pltpu.roll(fz, 255, 1) - pltpu.roll(fz, 1, 1))[:, 0:128]
    return 0.25 * (fx[x + 2] - fx[x] + dy + dz)


def blocks(ref):
    return jnp.concatenate([ref[n].T for n in range(8)], 0)


def column_wide(values):
    return jnp.concatenate([jnp.broadcast_to(values[:, z : z + 1], (64, 256)) for z in range(4)], 0)


def to_row(wide):
    return jnp.sum(jnp.where(iota((256, 256), 0) == iota((256, 256), 1), wide, 0.0), axis=0, keepdims=True)


def first_kernel(sizes, act_ref, fi_ref, half_ref, slope_ref, tau_ref, cond_ref, rev_ref, angle, conduct, block_elem,
                 states_hbm, s1_hbm, xlo, xhi, ylo, yhi, msg, code_col, const, lines, states, s1, came, left, total, moment):
    pos_ref = place()
    coming = fetches(states_hbm, states, came)
    gate_constants(half_ref, slope_ref, tau_ref, cond_ref, rev_ref, const)
    ids = blocks(block_elem)
    owner = column_wide((ids // ELEMS).astype(F32))
    local = column_wide((ids % ELEMS).astype(F32))
    owner_row = to_row(owner)
    before = iota((256, 256), 1) < iota((256, 256), 0)
    rank = jnp.sum(jnp.where((owner == owner_row) & before, 1.0, 0.0), axis=1, keepdims=True)
    code = owner + 256.0 * rank
    code_col[...] = code[:, 0:128]
    row_code = to_row(code)
    local_row = to_row(local) + 1.0
    peers = iota((256, 256), 0).astype(F32)
    lane = iota((1, 128), 1)
    a, b = frame_of(angle), conduct[...]
    spread = b[0:1] - b[1:2]
    entries = [b[1:2] + spread * a[n] * a[n] for n in range(3)]
    entries += [spread * a[0] * a[1], spread * a[0] * a[2], spread * a[1] * a[2]]
    head = jnp.zeros((1, 128), F32)
    slots = iota((1, NF), 1)
    for tile in range(2):
        alive = (act_ref[tile] > 0).astype(F32)
        chosen = slots == fi_ref[tile]
        for n in range(6):
            value = jnp.sum(jnp.where(chosen, entries[n], 0.0), axis=1, keepdims=True) * alive
            head = jnp.where(lane == HEAD + 7 * tile + n, value, head)
        head = jnp.where(lane == HEAD + 7 * tile + 6, alive, head)
    asked = jnp.broadcast_to(head, (256, 128))
    target = iota((128, 256), 0)
    for r in range(2):
        goes = (row_code == peers + 256.0 * r).astype(F32).astype(BF16)
        labels = jnp.where(target == r, local_row, 0.0).astype(BF16)
        asked += lax.dot_general(goes, labels, NT, preferred_element_type=F32)
    msg[...] = jnp.zeros((ROWS * 256, 128), F32)
    msg[FIRST, :] = asked
    alive = [act_ref[half] > 0 for half in range(2)]
    leaving = ionic_step(states.at[0], states, s1, alive, const, total, moment, coming, s1_hbm, left)
    send_faces(s1.at[0], pos_ref, sizes, xlo, xhi, ylo, yhi, msg, lines)
    for copy in leaving:
        copy.wait()


def element_kernel(material, angle, node_disp, elem_node, elem_fibre, corner, passive, active):
    table = jnp.concatenate([*frame_of(angle), jnp.zeros((5, NF), F32)], 0)
    hot = (iota((NF, ELEMS), 0) == elem_fibre[...]).astype(F32)
    fibre = jnp.dot(table, hot, precision=HIGHEST, preferred_element_type=F32)
    f = [fibre[j : j + 1] for j in range(3)]
    disp = jnp.concatenate([node_disp[...], jnp.zeros((5, NODES), F32)], 0)
    packed = jnp.concatenate([p.astype(F32) for p in parts3(disp)] + [jnp.zeros((8, NODES), F32)], 0).astype(BF16)
    slope = [jnp.zeros((8, ELEMS), F32) for _ in range(3)]
    for q in range(8):
        hot = (iota((NODES, ELEMS), 0) == elem_node[q : q + 1, :]).astype(F32).astype(BF16)
        got = jnp.dot(packed, hot, preferred_element_type=F32)
        got = got[0:8] + got[8:16] + got[16:24]
        corner[8 * q : 8 * q + 8] = got
        for j in range(3):
            slope[j] += got if CORNERS[q][j] else -got
    F = [[slope[j][i : i + 1] * 0.25 + (1.0 if i == j else 0.0) for j in range(3)] for i in range(3)]

    def cofactor(i, j):
        a, b = [n for n in range(3) if n != i]
        c, d = [n for n in range(3) if n != j]
        minor = F[a][c] * F[b][d] - F[a][d] * F[b][c]
        return minor if (i + j) % 2 == 0 else -minor

    cof = [[cofactor(i, j) for j in range(3)] for i in range(3)]
    volume = F[0][0] * cof[0][0] + F[0][1] * cof[0][1] + F[0][2] * cof[0][2]
    invert = 1.0 / volume
    bulk = material[1] * jnp.log(volume)
    none = jnp.zeros((5, ELEMS), F32)
    stress, fibres = [], []
    stretch = [F[i][0] * f[0] + F[i][1] * f[1] + F[i][2] * f[2] for i in range(3)]
    for j in range(3):
        rows = []
        for i in range(3):
            inverse = cof[i][j] * invert
            rows.append(material[0] * (F[i][j] - inverse) + bulk * inverse)
        stress.append(jnp.concatenate([*rows, none], 0))
        fibres.append(jnp.concatenate([*[material[2] * stretch[i] * f[j] for i in range(3)], none], 0))
    total = jnp.zeros((24, NODES), F32)
    for q in range(8):
        sign = [0.25 if CORNERS[q][j] else -0.25 for j in range(3)]
        force = stress[0] * sign[0] + stress[1] * sign[1] + stress[2] * sign[2]
        active[8 * q : 8 * q + 8] = fibres[0] * sign[0] + fibres[1] * sign[1] + fibres[2] * sign[2]
        hot = (iota((NODES, ELEMS), 0) == elem_node[q : q + 1, :]).astype(F32).astype(BF16)
        packed = jnp.concatenate([p.astype(F32) for p in parts3(force)], 0).astype(BF16)
        total += lax.dot_general(packed, hot, NT, preferred_element_type=F32)
    passive[...] = total[0:8] + total[8:16] + total[16:24]


def second_kernel(sizes, half_ref, slope_ref, tau_ref, cond_ref, rev_ref, s1_hbm, xm, xp, ym, yp, got1, corner,
                  code_col, block_weight, s2_hbm, xlo, xhi, ylo, yhi, msg, heard, const, lines, s1, s2, came, left, total, moment, vext, fx, cx, cy, cz,
                  tens):
    pos_ref = place()
    coming = fetches(s1_hbm, s1, came)
    gate_constants(half_ref, slope_ref, tau_ref, cond_ref, rev_ref, const)
    heard[...] = got1[FIRST, :]
    live = tile_planes(pos_ref, sizes, heard, cx, cy, cz)
    coming[0].wait()
    fill_extended(vext, s1.at[0], (xm, xp, ym, yp), got1, pos_ref, sizes)
    flux_x(vext, fx, cx)

    @pl.loop(0, CX, unroll=4)
    def _(x):
        here = jnp.where(x < 8, live[0], live[1])
        tens[x] = s1[0, x] + here * lap_plane(vext, fx, cy, cz, x)

    alive = [jnp.broadcast_to(here, (16, 128)) > 0.5 for here in live]
    leaving = ionic_step(tens, s1, s2, alive, const, total, moment, [None, *coming[1:]], s2_hbm, left)
    for n in range(8):
        ratio = jnp.zeros((16, 128), F32)
        for x in (2 * n, 2 * n + 1):
            square = s2[NSTATE - 1, x] * s2[NSTATE - 1, x]
            ratio += square / (square + 0.09)
        lines[16 * n : 16 * n + 16] = ratio
    pairs = lines[...]
    row, lane = iota((64, 128), 0), iota((64, 128), 1)
    over_y = ((row // 8 == lane // 16) & (row % 8 == lane % 16 // 2)).astype(F32)
    over_z = jnp.where(iota((128, 128), 0) // 32 == iota((128, 128), 1), 1.0 / 128.0, 0.0)
    mean = jnp.dot(over_y, pairs, precision=HIGHEST, preferred_element_type=F32)
    mean = jnp.dot(mean, over_z, precision=HIGHEST, preferred_element_type=F32)
    value = to_row(column_wide(mean[:, 0:4] * blocks(block_weight)))
    peers = iota((256, 256), 0).astype(F32)
    elems = iota((256, 256), 1).astype(F32)
    row_code = to_row(jnp.concatenate([code_col[...], code_col[...]], 1))
    target = iota((128, 256), 0)
    answer = jnp.zeros((256, 128), F32)
    asked = heard[...]
    none = jnp.zeros((64, 256), F32)
    for r in range(2):
        goes = (row_code == peers + 256.0 * r).astype(F32).astype(BF16)
        for part in parts3(jnp.where(target == 64 * r + 3, value, 0.0)):
            answer += lax.dot_general(goes, part, NT, preferred_element_type=F32)
        wants = (asked[:, r : r + 1] == elems + 1.0).astype(F32).astype(BF16)
        held = jnp.concatenate([corner[...], none] if r == 0 else [none, corner[...]], 0)
        for part in parts3(held)[:2]:
            answer += lax.dot_general(wants, part, NT, preferred_element_type=F32)
    msg[...] = jnp.zeros((ROWS * 256, 128), F32)
    msg[FIRST, :] = answer
    send_faces(s2.at[0], pos_ref, sizes, xlo, xhi, ylo, yhi, msg, lines)
    for copy in leaving:
        copy.wait()


def third_kernel(sizes, s2, xm, xp, ym, yp, heard, got2, code_col, elem_node, passive, active, blend_hbm, s3, fine,
                 residual, vext, fx, cx, cy, cz, blend, came):
    pos_ref = place()
    coming = pltpu.make_async_copy(blend_hbm, blend, came)
    coming.start()
    live = tile_planes(pos_ref, sizes, heard, cx, cy, cz)
    fill_extended(vext, s2.at[0], (xm, xp, ym, yp), got2, pos_ref, sizes)
    flux_x(vext, fx, cx)

    @pl.loop(0, CX, unroll=4)
    def _(x):
        here = jnp.where(x < 8, live[0], live[1])
        s3[0, x] = s2[0, x] + here * lap_plane(vext, fx, cy, cz, x)

    elems = iota((256, 256), 1).astype(F32)
    tension = jnp.zeros((1, 256), F32)
    asked, answer = heard[...], got2[FIRST, :]
    for r in range(2):
        wants = asked[:, r : r + 1] == elems + 1.0
        tension += jnp.sum(jnp.where(wants, answer[:, 64 * r + 3 : 64 * r + 4], 0.0), axis=0, keepdims=True)
    total = jnp.zeros((24, NODES), F32)
    for q in range(8):
        hot = (iota((NODES, ELEMS), 0) == elem_node[q : q + 1, :]).astype(F32).astype(BF16)
        packed = jnp.concatenate([p.astype(F32) for p in parts3(active[8 * q : 8 * q + 8] * tension)], 0).astype(BF16)
        total += lax.dot_general(packed, hot, NT, preferred_element_type=F32)
    total = passive[...] + total[0:8] + total[8:16] + total[16:24]
    residual[...] = total[0:3]

    code = jnp.concatenate([code_col[...], code_col[...]], 1)
    lane = iota((256, 128), 1)
    disp = jnp.zeros((256, 128), F32)
    for r in range(2):
        goes = (code == elems + 256.0 * r).astype(F32).astype(BF16)
        part = jnp.where(lane // 64 == r, answer, 0.0)
        part = part if r == 0 else pltpu.roll(part, 64, 1)
        for piece in parts3(part)[:2]:
            disp += jnp.dot(goes, piece, preferred_element_type=F32)
    merged = jnp.concatenate(
        [disp[0:64] + pltpu.roll(disp[64:128], 64, 1), disp[128:192] + pltpu.roll(disp[192:256], 64, 1)], 1
    )
    which = iota((64, 256), 1) % 8
    rows = jnp.concatenate([jnp.where(which == c, merged, 0.0) for c in range(3)], 0)
    first, second, _ = parts3(rows)
    coming.wait()
    out = jnp.dot(first, blend[0], preferred_element_type=F32) + jnp.dot(second, blend[0], preferred_element_type=F32)
    out += jnp.dot(first, blend[1], preferred_element_type=F32)
    for c in range(3):
        for bx in range(8):
            tile = out[64 * c + 8 * bx : 64 * c + 8 * bx + 8]
            for i in range(2):
                for j in range(2):
                    at = 128 * (2 * i + j)
                    fine[c, 2 * bx + i, pl.ds(j, 8, stride=2), :] = tile[:, at : at + 128]


def blend_table():
    table = np.zeros((4, 8, 8, 2, 2, 128), np.float64)
    z = np.arange(128)
    for q, bits in enumerate(CORNERS):
        for i in range(2):
            for j in range(2):
                for bz in range(4):
                    xi = ((i + 0.5) / 2, (j + 0.5) / 2, (z % 32 + 0.5) / 32)
                    w = 1.0
                    for d in range(3):
                        w = w * (xi[d] if bits[d] else 1.0 - xi[d])
                    table[bz, q, :, i, j] = w * (z // 32 == bz)
    table = table.reshape(256, 512)
    import ml_dtypes

    first = table.astype(ml_dtypes.bfloat16)
    second = (table - first.astype(np.float64)).astype(ml_dtypes.bfloat16)
    return np.stack([first, second])


def shift(x, axis, by):
    count = lax.axis_size(axis)
    pairs = [(i, i + by) for i in range(count) if 0 <= i + by < count]
    return lax.ppermute(x, axis, pairs)


def exchange(xlo, xhi, ylo, yhi, msg):
    got = lax.all_to_all(msg.reshape(256, 1, ROWS * 128), ALL, 0, 0, tiled=True).reshape(ROWS * 256, 128)
    halo = shift(xhi, "gx", 1), shift(xlo, "gx", -1), shift(yhi, "gy", 1), shift(ylo, "gy", -1)
    return halo, got


def whole(shape, space=None):
    return pl.BlockSpec(shape, lambda i: (0,) * len(shape), memory_space=space)


ANYWHERE = pl.BlockSpec(memory_space=pl.ANY)


def call(body, name, scalars, arrays, outs, scratch=(), far=(), mebibytes=50):
    specs = [ANYWHERE if n in far else whole(x.shape) for n, x in enumerate([*arrays, *outs])]
    return pl.pallas_call(
        body,
        grid=(1,),
        out_shape=outs,
        in_specs=[whole(x.shape, pltpu.SMEM) for x in scalars] + specs[: len(arrays)],
        out_specs=specs[len(arrays) :],
        scratch_shapes=scratch,
        compiler_params=grant(mebibytes),
        name=name,
    )(*scalars, *arrays)


def sds(*shape):
    return jax.ShapeDtypeStruct(shape, F32)


FACES = [sds(2, 16, 128), sds(2, 16, 128), sds(2, 16, 128), sds(2, 16, 128), sds(ROWS * 256, 128)]
STEP_SCRATCH = [
    pltpu.VMEM((20, 32, 256), F32),
    pltpu.VMEM((18, 16, 128), F32),
    pltpu.VMEM((4, 3, 16, 128), F32),
    pltpu.VMEM((2, 3, 32, 128), F32),
    pltpu.VMEM((2, 3, 16, 256), F32),
]
STATE_SCRATCH = [
    pltpu.VMEM((NSTATE, CX, CY, CZ), F32),
    pltpu.VMEM((NSTATE, CX, CY, CZ), F32),
    pltpu.SemaphoreType.DMA((len(GROUPS),)),
    pltpu.SemaphoreType.DMA((len(GROUPS),)),
    pltpu.VMEM((CX, CY, CZ), F32),
    pltpu.VMEM((CX, CY, CZ), F32),
]
GATE_SCRATCH = [pltpu.VMEM((6 * NCH, 8, 128), F32), pltpu.VMEM((128, 128), F32)]
def grant(mebibytes):
    return pltpu.CompilerParams(vmem_limit_bytes=mebibytes * 2**20)


def shards(states, active, fibre_index, fibre_angle, conduct, gate_half, gate_slope, gate_tau, conductance, reversal,
           block_elem, block_weight, node_disp, elem_node, elem_fibre, material):
    sizes = tuple(lax.axis_size(a) for a in ALL)
    gates = (gate_half, gate_slope, gate_tau, conductance, reversal)
    full = sds(NSTATE, CX, CY, CZ)
    s1, *faces, code_col = call(
        functools.partial(first_kernel, sizes),
        "first",
        (active.reshape(2), fibre_index.reshape(2), *gates),
        (fibre_angle, conduct, block_elem.transpose(0, 2, 1), states),
        [full, *FACES, sds(256, 128)],
        GATE_SCRATCH + STATE_SCRATCH,
        (3, 4),
        60,
    )
    halo, got1 = exchange(*faces)
    corner, passive, active_force = call(
        element_kernel,
        "elements",
        (material,),
        (fibre_angle, node_disp, elem_node, elem_fibre.reshape(1, ELEMS)),
        [sds(64, ELEMS), sds(8, NODES), sds(64, ELEMS)],
    )
    s2, *faces, heard = call(
        functools.partial(second_kernel, sizes),
        "second",
        gates,
        (s1, *halo, got1, corner, code_col, block_weight.transpose(0, 2, 1)),
        [full, *FACES, sds(256, 128)],
        GATE_SCRATCH + STATE_SCRATCH + STEP_SCRATCH + [pltpu.VMEM((16, 16, 128), F32)],
        (0, 9),
    )
    halo, got2 = exchange(*faces)
    plane = whole((1, CX, CY, CZ))
    blend = jnp.asarray(blend_table())
    rest = (*halo, heard, got2, code_col, elem_node, passive, active_force)
    outs = [full, sds(3, CX, CY, CZ), sds(3, NODES)]
    return pl.pallas_call(
        functools.partial(third_kernel, sizes),
        grid=(1,),
        out_shape=outs,
        in_specs=[plane, *[whole(x.shape) for x in rest], ANYWHERE],
        out_specs=[plane, whole(outs[1].shape), whole(outs[2].shape)],
        scratch_shapes=STEP_SCRATCH + [pltpu.VMEM(blend.shape, BF16), pltpu.SemaphoreType.DMA],
        input_output_aliases={0: 0},
        compiler_params=grant(50),
        name="third",
    )(s2, *rest, blend)


def solution(mesh):
    in_specs = (
        P(None, "gx", "gy", "gz"),
        *[P("gx", "gy", "gz")] * 2,
        *[P()] * 7,
        *[P("gx", "gy", "gz")] * 2,
        *[P(None, ALL)] * 2,
        P(ALL),
        P(),
    )
    out_specs = (P(None, "gx", "gy", "gz"), P(None, "gx", "gy", "gz"), P(None, ALL))
    return jax.shard_map(shards, mesh=mesh, in_specs=in_specs, out_specs=out_specs, check_vma=False)
```

```python
import functools

import jax
import jax.numpy as jnp
import numpy as np
from jax import lax
from jax.experimental import pallas as pl
from jax.experimental.pallas import tpu as pltpu
from jax.sharding import PartitionSpec as P

NSTATE, NCH, NF = 19, 17, 64
CX, CY, CZ = 16, 16, 128
ELEMS, SLOTS, NODES = 256, 256, 512
ALL = ("gx", "gy", "gz")
HIGHEST = lax.Precision.HIGHEST
F32, BF16 = jnp.float32, jnp.bfloat16
NT = (((1,), (1,)), ((), ()))
TN = (((0,), (0,)), ((), ()))
CORNERS = [(q // 4, q // 2 % 2, q % 2) for q in range(8)]
HEAD = 2


def iota(shape, dim):
    return lax.broadcasted_iota(jnp.int32, shape, dim)


def place():
    return [lax.axis_index(a) for a in ALL]


def neighbour(pos_ref, sizes, step):
    at = [pos_ref[d] + step[d] for d in range(3)]
    ok = (at[0] >= 0) & (at[0] < sizes[0])
    for d in (1, 2):
        ok = ok & (at[d] >= 0) & (at[d] < sizes[d])
    row = (at[0] * sizes[1] + at[1]) * sizes[2] + at[2]
    return jnp.where(ok, row, 0), ok


ROWS = 5
FIRST = pl.ds(0, 256, stride=ROWS)


def put_row(msg, peer, ok, values, place=1):
    row = ROWS * peer + place
    base = pl.ds(pl.multiple_of(row // 8 * 8, 8), 8)
    here = iota((8, 128), 0) == jnp.where(ok, row % 8, -1)
    pltpu.store(msg.at[base, :], jnp.broadcast_to(values, (8, 128)), mask=here)


def take_row(got, peer, ok, place, rows_each=ROWS):
    row = rows_each * peer + place
    rows = got[pl.ds(pl.multiple_of(row // 8 * 8, 8), 8), :]
    here = iota((8, 128), 0) == jnp.where(ok, row % 8, -1)
    return jnp.sum(jnp.where(here, rows, 0.0), axis=0, keepdims=True)


def parts3(x):
    first = x.astype(BF16)
    rest = x - first.astype(F32)
    second = rest.astype(BF16)
    third = (rest - second.astype(F32)).astype(BF16)
    return first, second, third


def frame_of(angles):
    a, b = angles[0:1, :], angles[1:2, :]
    return jnp.cos(a) * jnp.cos(b), jnp.sin(a) * jnp.cos(b), jnp.sin(b)


def gate_constants(half_ref, slope_ref, tau_ref, cond_ref, rev_ref, const):
    for c in range(NCH):
        scale = 0.5 / jnp.full((8, 128), slope_ref[c], F32)
        keep = jnp.exp(-1.0 / jnp.full((8, 128), tau_ref[c], F32))
        cond = jnp.full((8, 128), cond_ref[c], F32)
        const[c] = scale
        const[NCH + c] = -half_ref[c] * scale
        const[2 * NCH + c] = keep
        const[3 * NCH + c] = 0.5 * (1.0 - keep)
        const[4 * NCH + c] = cond
        const[5 * NCH + c] = cond * rev_ref[c]


GROUPS = ((0, 1), (1, 5), (5, 9), (9, 13), (13, 17), (17, NSTATE))


def fetches(hbm, vmem, sems):
    copies = []
    for n, (low, high) in enumerate(GROUPS):
        copies.append(pltpu.make_async_copy(hbm.at[low:high], vmem.at[low:high], sems.at[n]))
        copies[n].start()
    return copies


def drain(vmem, hbm, sems, n):
    low, high = GROUPS[n]
    copy = pltpu.make_async_copy(vmem.at[low:high], hbm.at[low:high], sems.at[n])
    copy.start()
    return copy


def twice(x):
    return jnp.concatenate([x, x], 0)


def ionic_step(volt, source, target, alive, const, total, moment, coming, hbm, left):
    leaving = []
    for n, (low, high) in enumerate(GROUPS):
        if coming[n] is not None:
            coming[n].wait()
        for s in range(max(low, 1), high):
            c = s - 1
            for half in range(2):

                @pl.loop(8 * half, 8 * half + 8, unroll=8)
                def _(x):
                    old = source[s, x]
                    if s < NSTATE - 1:
                        rise = jnp.tanh(volt[x] * twice(const[c]) + twice(const[NCH + c]))
                        lift = twice(const[3 * NCH + c])
                        new = old * twice(const[2 * NCH + c]) + (lift * rise + lift)
                        flow, shift_ = new * twice(const[4 * NCH + c]), new * twice(const[5 * NCH + c])
                        total[x] = flow if c == 0 else total[x] + flow
                        moment[x] = shift_ if c == 0 else moment[x] + shift_
                    else:
                        new = old * 0.9 + 0.1 * (0.5 * jnp.tanh(4.0 * (volt[x] - 0.5)) + 0.5)
                    target[s, x] = jnp.where(alive[half], new, old)

        if n:
            leaving.append(drain(target, hbm, left, n))
    for half in range(2):

        @pl.loop(8 * half, 8 * half + 8, unroll=8)
        def _(x):
            v = volt[x]
            target[0, x] = jnp.where(alive[half], v - (v * total[x] - moment[x]), v)

    return [*leaving, drain(target, hbm, left, 0)]


def send_faces(v, pos_ref, sizes, xlo, xhi, ylo, yhi, msg, lines):
    xlo[...] = v[0:2]
    xhi[...] = v[14:16]
    for x in range(CX):
        for n in range(2):
            ylo[n, x : x + 1] = v[x, n : n + 1, :]
            yhi[n, x : x + 1] = v[x, 14 + n : 15 + n, :]
    row, lane = iota((8, 128), 0), iota((8, 128), 1)
    pick = ((row < 4) & (lane == jnp.where(row < 2, row, row + 124))).astype(F32)
    flat = v[...].reshape(CX * CY, CZ)
    ends = lax.dot_general(pick, flat, NT, precision=HIGHEST, preferred_element_type=F32)
    for dz in (-1, 1):
        peer, ok = neighbour(pos_ref, sizes, (0, 0, dz))
        for n in range(4):
            k, half = n // 2 + (2 if dz > 0 else 0), n % 2
            put_row(msg, peer, ok, ends[k : k + 1, 128 * half : 128 * half + 128], 1 + n)
    lines[0:16] = v[0]
    lines[16:32] = v[15]
    lines[32:48] = ylo[0]
    lines[48:64] = yhi[1]
    lines[64:128] = jnp.zeros((64, 128), F32)
    marks = lax.dot_general(pick, lines[...], NT, precision=HIGHEST, preferred_element_type=F32)
    for dx in (-1, 1):
        for dy in (-1, 1):
            peer, ok = neighbour(pos_ref, sizes, (dx, dy, 0))
            edge = v[15 if dx > 0 else 0, (15 if dy > 0 else 0) : (16 if dy > 0 else 1), :]

            put_row(msg, peer, ok, edge)

    for step in ((-1, 0), (1, 0), (0, -1), (0, 1)):
        for dz in (-1, 1):
            peer, ok = neighbour(pos_ref, sizes, (*step, dz))
            edge = marks[3:4] if dz > 0 else marks[0:1]

            put_row(msg, peer, ok, edge)


def heads(pos_ref, sizes, got, step):
    row, ok = neighbour(pos_ref, sizes, step)
    return take_row(got, row, ok, 0, 1)


def entry(head, tile, which):
    lane = HEAD + 7 * tile + which
    return head[:, lane : lane + 1]


def edges_of(pos_ref, sizes, got, step):
    row, ok = neighbour(pos_ref, sizes, step)
    return take_row(got, row, ok, 1)


def tile_planes(pos_ref, sizes, got1, cx, cy, cz):
    own = heads(pos_ref, sizes, got1, (0, 0, 0))
    ends = {s: heads(pos_ref, sizes, got1, s) for s in ((-1, 0, 0), (1, 0, 0), (0, -1, 0), (0, 1, 0), (0, 0, -1), (0, 0, 1))}
    for k, (head, tile) in enumerate(((ends[-1, 0, 0], 1), (own, 0), (own, 1), (ends[1, 0, 0], 0))):
        for n, which in enumerate((0, 3, 4)):
            cx[k, n] = jnp.broadcast_to(entry(head, tile, which), (16, 128))
    rows, lanes = iota((32, 128), 0), iota((16, 256), 1)
    for tile in range(2):
        for n, which in enumerate((3, 1, 5)):
            cy[tile, n] = jnp.where(
                rows == 7,
                entry(ends[0, -1, 0], tile, which),
                jnp.where(rows == 24, entry(ends[0, 1, 0], tile, which), entry(own, tile, which)),
            )
        for n, which in enumerate((4, 5, 2)):
            cz[tile, n] = jnp.where(
                lanes == 255,
                entry(ends[0, 0, -1], tile, which),
                jnp.where(lanes == 128, entry(ends[0, 0, 1], tile, which), entry(own, tile, which)),
            )
    return entry(own, 0, 6), entry(own, 1, 6)


def fill_extended(vext, v, faces, got, pos_ref, sizes):
    xm, xp, ym, yp = faces
    vext[2:18, 8:24, 0:128] = v[...]
    vext[0:2, 8:24, 0:128] = xm[...]
    vext[18:20, 8:24, 0:128] = xp[...]
    for x in range(CX):
        for n in range(2):
            vext[2 + x, 6 + n : 7 + n, 0:128] = ym[n, x : x + 1]
            vext[2 + x, 24 + n : 25 + n, 0:128] = yp[n, x : x + 1]
    row, lane = iota((8, 128), 0), iota((8, 128), 1)
    place = ((row < 4) & (lane == jnp.where(row < 2, row + 126, row - 2))).astype(F32)
    outer = []
    for dz in (-1, 1):
        peer, ok = neighbour(pos_ref, sizes, (0, 0, dz))
        for k in range(2):
            outer.append(jnp.concatenate([take_row(got, peer, ok, 1 + 2 * k + half) for half in range(2)], 1))
    outer = jnp.concatenate([*outer, jnp.zeros((4, 256), F32)], 0)
    beyond = lax.dot_general(outer, place, TN, precision=HIGHEST, preferred_element_type=F32)
    vext[2:18, 8:24, 128:256] = beyond.reshape(16, 16, 128)
    for dx, i in ((-1, 1), (1, 18)):
        for dy, j in ((-1, 7), (1, 24)):
            vext[i, j : j + 1, 0:128] = edges_of(pos_ref, sizes, got, (dx, dy, 0))
    lanes = iota((1, 128), 1)
    group = lanes // 16
    lines = []
    for dz in (-1, 1):
        line = jnp.zeros((1, 128), F32)
        for g, (dx, dy) in enumerate(((1, 0), (-1, 0), (0, 1), (0, -1))):
            line = jnp.where(group == g, edges_of(pos_ref, sizes, got, (dx, dy, dz)), line)
        lines.append(line)
    outer = jnp.concatenate([*lines, jnp.zeros((6, 128), F32)], 0)
    place = ((row < 2) & (lane == jnp.where(row == 0, 127, 0))).astype(F32)
    beyond = lax.dot_general(outer, place, TN, precision=HIGHEST, preferred_element_type=F32)
    vext[18, 8:24, 128:256] = beyond[0:16]
    vext[1, 8:24, 128:256] = beyond[16:32]
    for x in range(CX):
        vext[2 + x, 24:25, 128:256] = beyond[32 + x : 33 + x]
        vext[2 + x, 7:8, 128:256] = beyond[48 + x : 49 + x]


def flux_x(vext, fx, cx):
    def one(p, tile):
        wide = vext[p, 8:24, :]
        gx = vext[p + 1, 8:24, 0:128] - vext[p - 1, 8:24, 0:128]
        gy = vext[p, 9:25, 0:128] - vext[p, 7:23, 0:128]
        gz = (pltpu.roll(wide, 255, 1) - pltpu.roll(wide, 1, 1))[:, 0:128]
        fx[p - 1] = cx[tile, 0] * gx + cx[tile, 1] * gy + cx[tile, 2] * gz

    one(1, 0)
    one(18, 3)

    @pl.loop(2, 18, unroll=8)
    def _(p):
        one(p, jnp.where(p < 10, 1, 2))


def lap_plane(vext, fx, cy, cz, x):
    p = x + 2
    tile = x // 8
    wide = vext[p]
    gx = vext[p + 1] - vext[p - 1]
    gy = pltpu.roll(wide, 31, 0) - pltpu.roll(wide, 1, 0)
    gz = pltpu.roll(wide, 255, 1) - pltpu.roll(wide, 1, 1)
    fy = cy[tile, 0] * gx[:, 0:128] + cy[tile, 1] * gy[:, 0:128] + cy[tile, 2] * gz[:, 0:128]
    dy = (pltpu.roll(fy, 31, 0) - pltpu.roll(fy, 1, 0))[8:24]
    fz = cz[tile, 0] * gx[8:24] + cz[tile, 1] * gy[8:24] + cz[tile, 2] * gz[8:24]
    dz = (pltpu.roll(fz, 255, 1) - pltpu.roll(fz, 1, 1))[:, 0:128]
    return 0.25 * (fx[x + 2] - fx[x] + dy + dz)


def blocks(ref):
    return jnp.concatenate([ref[n].T for n in range(8)], 0)


def column_wide(values):
    return jnp.concatenate([jnp.broadcast_to(values[:, z : z + 1], (64, 256)) for z in range(4)], 0)


def to_row(wide):
    return jnp.sum(jnp.where(iota((256, 256), 0) == iota((256, 256), 1), wide, 0.0), axis=0, keepdims=True)


def first_kernel(sizes, act_ref, fi_ref, half_ref, slope_ref, tau_ref, cond_ref, rev_ref, angle, conduct, block_elem,
                 states_hbm, s1_hbm, xlo, xhi, ylo, yhi, msg, code_col, const, lines, states, s1, came, left, total, moment):
    pos_ref = place()
    coming = fetches(states_hbm, states, came)
    gate_constants(half_ref, slope_ref, tau_ref, cond_ref, rev_ref, const)
    ids = blocks(block_elem)
    owner = column_wide((ids // ELEMS).astype(F32))
    local = column_wide((ids % ELEMS).astype(F32))
    owner_row = to_row(owner)
    before = iota((256, 256), 1) < iota((256, 256), 0)
    rank = jnp.sum(jnp.where((owner == owner_row) & before, 1.0, 0.0), axis=1, keepdims=True)
    code = owner + 256.0 * rank
    code_col[...] = code[:, 0:128]
    row_code = to_row(code)
    local_row = to_row(local) + 1.0
    peers = iota((256, 256), 0).astype(F32)
    lane = iota((1, 128), 1)
    a, b = frame_of(angle), conduct[...]
    spread = b[0:1] - b[1:2]
    entries = [b[1:2] + spread * a[n] * a[n] for n in range(3)]
    entries += [spread * a[0] * a[1], spread * a[0] * a[2], spread * a[1] * a[2]]
    head = jnp.zeros((1, 128), F32)
    slots = iota((1, NF), 1)
    for tile in range(2):
        alive = (act_ref[tile] > 0).astype(F32)
        chosen = slots == fi_ref[tile]
        for n in range(6):
            value = jnp.sum(jnp.where(chosen, entries[n], 0.0), axis=1, keepdims=True) * alive
            head = jnp.where(lane == HEAD + 7 * tile + n, value, head)
        head = jnp.where(lane == HEAD + 7 * tile + 6, alive, head)
    asked = jnp.broadcast_to(head, (256, 128))
    target = iota((128, 256), 0)
    for r in range(2):
        goes = (row_code == peers + 256.0 * r).astype(F32).astype(BF16)
        labels = jnp.where(target == r, local_row, 0.0).astype(BF16)
        asked += lax.dot_general(goes, labels, NT, preferred_element_type=F32)
    msg[...] = jnp.zeros((ROWS * 256, 128), F32)
    msg[FIRST, :] = asked
    alive = [act_ref[half] > 0 for half in range(2)]
    leaving = ionic_step(states.at[0], states, s1, alive, const, total, moment, coming, s1_hbm, left)
    send_faces(s1.at[0], pos_ref, sizes, xlo, xhi, ylo, yhi, msg, lines)
    for copy in leaving:
        copy.wait()


def element_kernel(material, angle, node_disp, elem_node, elem_fibre, corner, passive, active):
    table = jnp.concatenate([*frame_of(angle), jnp.zeros((5, NF), F32)], 0)
    hot = (iota((NF, ELEMS), 0) == elem_fibre[...]).astype(F32)
    fibre = jnp.dot(table, hot, precision=HIGHEST, preferred_element_type=F32)
    f = [fibre[j : j + 1] for j in range(3)]
    disp = jnp.concatenate([node_disp[...], jnp.zeros((5, NODES), F32)], 0)
    packed = jnp.concatenate([p.astype(F32) for p in parts3(disp)] + [jnp.zeros((8, NODES), F32)], 0).astype(BF16)
    slope = [jnp.zeros((8, ELEMS), F32) for _ in range(3)]
    for q in range(8):
        hot = (iota((NODES, ELEMS), 0) == elem_node[q : q + 1, :]).astype(F32).astype(BF16)
        got = jnp.dot(packed, hot, preferred_element_type=F32)
        got = got[0:8] + got[8:16] + got[16:24]
        corner[8 * q : 8 * q + 8] = got
        for j in range(3):
            slope[j] += got if CORNERS[q][j] else -got
    F = [[slope[j][i : i + 1] * 0.25 + (1.0 if i == j else 0.0) for j in range(3)] for i in range(3)]

    def cofactor(i, j):
        a, b = [n for n in range(3) if n != i]
        c, d = [n for n in range(3) if n != j]
        minor = F[a][c] * F[b][d] - F[a][d] * F[b][c]
        return minor if (i + j) % 2 == 0 else -minor

    cof = [[cofactor(i, j) for j in range(3)] for i in range(3)]
    volume = F[0][0] * cof[0][0] + F[0][1] * cof[0][1] + F[0][2] * cof[0][2]
    invert = 1.0 / volume
    bulk = material[1] * jnp.log(volume)
    none = jnp.zeros((5, ELEMS), F32)
    stress, fibres = [], []
    stretch = [F[i][0] * f[0] + F[i][1] * f[1] + F[i][2] * f[2] for i in range(3)]
    for j in range(3):
        rows = []
        for i in range(3):
            inverse = cof[i][j] * invert
            rows.append(material[0] * (F[i][j] - inverse) + bulk * inverse)
        stress.append(jnp.concatenate([*rows, none], 0))
        fibres.append(jnp.concatenate([*[material[2] * stretch[i] * f[j] for i in range(3)], none], 0))
    total = jnp.zeros((24, NODES), F32)
    for q in range(8):
        sign = [0.25 if CORNERS[q][j] else -0.25 for j in range(3)]
        force = stress[0] * sign[0] + stress[1] * sign[1] + stress[2] * sign[2]
        active[8 * q : 8 * q + 8] = fibres[0] * sign[0] + fibres[1] * sign[1] + fibres[2] * sign[2]
        hot = (iota((NODES, ELEMS), 0) == elem_node[q : q + 1, :]).astype(F32).astype(BF16)
        packed = jnp.concatenate([p.astype(F32) for p in parts3(force)], 0).astype(BF16)
        total += lax.dot_general(packed, hot, NT, preferred_element_type=F32)
    passive[...] = total[0:8] + total[8:16] + total[16:24]


def second_kernel(sizes, half_ref, slope_ref, tau_ref, cond_ref, rev_ref, s1_hbm, xm, xp, ym, yp, got1, corner,
                  code_col, block_weight, s2_hbm, xlo, xhi, ylo, yhi, msg, heard, const, lines, s1, s2, came, left, total, moment, vext, fx, cx, cy, cz,
                  tens):
    pos_ref = place()
    coming = fetches(s1_hbm, s1, came)
    gate_constants(half_ref, slope_ref, tau_ref, cond_ref, rev_ref, const)
    heard[...] = got1[FIRST, :]
    live = tile_planes(pos_ref, sizes, heard, cx, cy, cz)
    coming[0].wait()
    fill_extended(vext, s1.at[0], (xm, xp, ym, yp), got1, pos_ref, sizes)
    flux_x(vext, fx, cx)

    @pl.loop(0, CX, unroll=8)
    def _(x):
        here = jnp.where(x < 8, live[0], live[1])
        tens[x] = s1[0, x] + here * lap_plane(vext, fx, cy, cz, x)

    alive = [jnp.broadcast_to(here, (16, 128)) > 0.5 for here in live]
    leaving = ionic_step(tens, s1, s2, alive, const, total, moment, [None, *coming[1:]], s2_hbm, left)
    for n in range(8):
        ratio = jnp.zeros((16, 128), F32)
        for x in (2 * n, 2 * n + 1):
            square = s2[NSTATE - 1, x] * s2[NSTATE - 1, x]
            ratio += square / (square + 0.09)
        lines[16 * n : 16 * n + 16] = ratio
    pairs = lines[...]
    row, lane = iota((64, 128), 0), iota((64, 128), 1)
    over_y = ((row // 8 == lane // 16) & (row % 8 == lane % 16 // 2)).astype(F32)
    over_z = jnp.where(iota((128, 128), 0) // 32 == iota((128, 128), 1), 1.0 / 128.0, 0.0)
    mean = jnp.dot(over_y, pairs, precision=HIGHEST, preferred_element_type=F32)
    mean = jnp.dot(mean, over_z, precision=HIGHEST, preferred_element_type=F32)
    value = to_row(column_wide(mean[:, 0:4] * blocks(block_weight)))
    peers = iota((256, 256), 0).astype(F32)
    elems = iota((256, 256), 1).astype(F32)
    row_code = to_row(jnp.concatenate([code_col[...], code_col[...]], 1))
    target = iota((128, 256), 0)
    answer = jnp.zeros((256, 128), F32)
    asked = heard[...]
    none = jnp.zeros((64, 256), F32)
    for r in range(2):
        goes = (row_code == peers + 256.0 * r).astype(F32).astype(BF16)
        for part in parts3(jnp.where(target == 64 * r + 3, value, 0.0)):
            answer += lax.dot_general(goes, part, NT, preferred_element_type=F32)
        wants = (asked[:, r : r + 1] == elems + 1.0).astype(F32).astype(BF16)
        held = jnp.concatenate([corner[...], none] if r == 0 else [none, corner[...]], 0)
        for part in parts3(held)[:2]:
            answer += lax.dot_general(wants, part, NT, preferred_element_type=F32)
    msg[...] = jnp.zeros((ROWS * 256, 128), F32)
    msg[FIRST, :] = answer
    send_faces(s2.at[0], pos_ref, sizes, xlo, xhi, ylo, yhi, msg, lines)
    for copy in leaving:
        copy.wait()


def third_kernel(sizes, s2, xm, xp, ym, yp, heard, got2, code_col, elem_node, passive, active, blend_hbm, s3, fine,
                 residual, vext, fx, cx, cy, cz, blend, came):
    pos_ref = place()
    coming = pltpu.make_async_copy(blend_hbm, blend, came)
    coming.start()
    live = tile_planes(pos_ref, sizes, heard, cx, cy, cz)
    fill_extended(vext, s2.at[0], (xm, xp, ym, yp), got2, pos_ref, sizes)
    flux_x(vext, fx, cx)

    @pl.loop(0, CX, unroll=8)
    def _(x):
        here = jnp.where(x < 8, live[0], live[1])
        s3[0, x] = s2[0, x] + here * lap_plane(vext, fx, cy, cz, x)

    elems = iota((256, 256), 1).astype(F32)
    tension = jnp.zeros((1, 256), F32)
    asked, answer = heard[...], got2[FIRST, :]
    for r in range(2):
        wants = asked[:, r : r + 1] == elems + 1.0
        tension += jnp.sum(jnp.where(wants, answer[:, 64 * r + 3 : 64 * r + 4], 0.0), axis=0, keepdims=True)
    total = jnp.zeros((16, NODES), F32)
    for q in range(8):
        hot = (iota((NODES, ELEMS), 0) == elem_node[q : q + 1, :]).astype(F32).astype(BF16)
        packed = jnp.concatenate([p.astype(F32) for p in parts3(active[8 * q : 8 * q + 8] * tension)[:2]], 0).astype(BF16)
        total += lax.dot_general(packed, hot, NT, preferred_element_type=F32)
    total = passive[...] + total[0:8] + total[8:16]
    residual[...] = total[0:3]

    code = jnp.concatenate([code_col[...], code_col[...]], 1)
    lane = iota((256, 128), 1)
    disp = jnp.zeros((256, 128), F32)
    for r in range(2):
        goes = (code == elems + 256.0 * r).astype(F32).astype(BF16)
        part = jnp.where(lane // 64 == r, answer, 0.0)
        part = part if r == 0 else pltpu.roll(part, 64, 1)
        for piece in parts3(part)[:2]:
            disp += jnp.dot(goes, piece, preferred_element_type=F32)
    merged = jnp.concatenate(
        [disp[0:64] + pltpu.roll(disp[64:128], 64, 1), disp[128:192] + pltpu.roll(disp[192:256], 64, 1)], 1
    )
    which = iota((64, 256), 1) % 8
    rows = jnp.concatenate([jnp.where(which == c, merged, 0.0) for c in range(3)], 0)
    first, second, _ = parts3(rows)
    coming.wait()
    out = jnp.dot(first, blend[0], preferred_element_type=F32) + jnp.dot(second, blend[0], preferred_element_type=F32)
    out += jnp.dot(first, blend[1], preferred_element_type=F32)
    for c in range(3):
        for bx in range(8):
            tile = out[64 * c + 8 * bx : 64 * c + 8 * bx + 8]
            for i in range(2):
                for j in range(2):
                    at = 128 * (2 * i + j)
                    fine[c, 2 * bx + i, pl.ds(j, 8, stride=2), :] = tile[:, at : at + 128]


def blend_table():
    table = np.zeros((4, 8, 8, 2, 2, 128), np.float64)
    z = np.arange(128)
    for q, bits in enumerate(CORNERS):
        for i in range(2):
            for j in range(2):
                for bz in range(4):
                    xi = ((i + 0.5) / 2, (j + 0.5) / 2, (z % 32 + 0.5) / 32)
                    w = 1.0
                    for d in range(3):
                        w = w * (xi[d] if bits[d] else 1.0 - xi[d])
                    table[bz, q, :, i, j] = w * (z // 32 == bz)
    table = table.reshape(256, 512)
    import ml_dtypes

    first = table.astype(ml_dtypes.bfloat16)
    second = (table - first.astype(np.float64)).astype(ml_dtypes.bfloat16)
    return np.stack([first, second])


def shift(x, axis, by):
    count = lax.axis_size(axis)
    pairs = [(i, i + by) for i in range(count) if 0 <= i + by < count]
    return lax.ppermute(x, axis, pairs)


def exchange(xlo, xhi, ylo, yhi, msg):
    got = lax.all_to_all(msg.reshape(256, 1, ROWS * 128), ALL, 0, 0, tiled=True).reshape(ROWS * 256, 128)
    halo = shift(xhi, "gx", 1), shift(xlo, "gx", -1), shift(yhi, "gy", 1), shift(ylo, "gy", -1)
    return halo, got


def whole(shape, space=None):
    return pl.BlockSpec(shape, lambda i: (0,) * len(shape), memory_space=space)


ANYWHERE = pl.BlockSpec(memory_space=pl.ANY)


def call(body, name, scalars, arrays, outs, scratch=(), far=(), mebibytes=50):
    specs = [ANYWHERE if n in far else whole(x.shape) for n, x in enumerate([*arrays, *outs])]
    return pl.pallas_call(
        body,
        grid=(1,),
        out_shape=outs,
        in_specs=[whole(x.shape, pltpu.SMEM) for x in scalars] + specs[: len(arrays)],
        out_specs=specs[len(arrays) :],
        scratch_shapes=scratch,
        compiler_params=grant(mebibytes),
        name=name,
    )(*scalars, *arrays)


def sds(*shape):
    return jax.ShapeDtypeStruct(shape, F32)


FACES = [sds(2, 16, 128), sds(2, 16, 128), sds(2, 16, 128), sds(2, 16, 128), sds(ROWS * 256, 128)]
STEP_SCRATCH = [
    pltpu.VMEM((20, 32, 256), F32),
    pltpu.VMEM((18, 16, 128), F32),
    pltpu.VMEM((4, 3, 16, 128), F32),
    pltpu.VMEM((2, 3, 32, 128), F32),
    pltpu.VMEM((2, 3, 16, 256), F32),
]
STATE_SCRATCH = [
    pltpu.VMEM((NSTATE, CX, CY, CZ), F32),
    pltpu.VMEM((NSTATE, CX, CY, CZ), F32),
    pltpu.SemaphoreType.DMA((len(GROUPS),)),
    pltpu.SemaphoreType.DMA((len(GROUPS),)),
    pltpu.VMEM((CX, CY, CZ), F32),
    pltpu.VMEM((CX, CY, CZ), F32),
]
GATE_SCRATCH = [pltpu.VMEM((6 * NCH, 8, 128), F32), pltpu.VMEM((128, 128), F32)]
def grant(mebibytes):
    return pltpu.CompilerParams(vmem_limit_bytes=mebibytes * 2**20)


def shards(states, active, fibre_index, fibre_angle, conduct, gate_half, gate_slope, gate_tau, conductance, reversal,
           block_elem, block_weight, node_disp, elem_node, elem_fibre, material):
    sizes = tuple(lax.axis_size(a) for a in ALL)
    gates = (gate_half, gate_slope, gate_tau, conductance, reversal)
    full = sds(NSTATE, CX, CY, CZ)
    s1, *faces, code_col = call(
        functools.partial(first_kernel, sizes),
        "first",
        (active.reshape(2), fibre_index.reshape(2), *gates),
        (fibre_angle, conduct, block_elem.transpose(0, 2, 1), states),
        [full, *FACES, sds(256, 128)],
        GATE_SCRATCH + STATE_SCRATCH,
        (3, 4),
        60,
    )
    halo, got1 = exchange(*faces)
    corner, passive, active_force = call(
        element_kernel,
        "elements",
        (material,),
        (fibre_angle, node_disp, elem_node, elem_fibre.reshape(1, ELEMS)),
        [sds(64, ELEMS), sds(8, NODES), sds(64, ELEMS)],
    )
    s2, *faces, heard = call(
        functools.partial(second_kernel, sizes),
        "second",
        gates,
        (s1, *halo, got1, corner, code_col, block_weight.transpose(0, 2, 1)),
        [full, *FACES, sds(256, 128)],
        GATE_SCRATCH + STATE_SCRATCH + STEP_SCRATCH + [pltpu.VMEM((16, 16, 128), F32)],
        (0, 9),
    )
    halo, got2 = exchange(*faces)
    plane = whole((1, CX, CY, CZ))
    blend = jnp.asarray(blend_table())
    rest = (*halo, heard, got2, code_col, elem_node, passive, active_force)
    outs = [full, sds(3, CX, CY, CZ), sds(3, NODES)]
    return pl.pallas_call(
        functools.partial(third_kernel, sizes),
        grid=(1,),
        out_shape=outs,
        in_specs=[plane, *[whole(x.shape) for x in rest], ANYWHERE],
        out_specs=[plane, whole(outs[1].shape), whole(outs[2].shape)],
        scratch_shapes=STEP_SCRATCH + [pltpu.VMEM(blend.shape, BF16), pltpu.SemaphoreType.DMA],
        input_output_aliases={0: 0},
        compiler_params=grant(50),
        name="third",
    )(s2, *rest, blend)


def solution(mesh):
    in_specs = (
        P(None, "gx", "gy", "gz"),
        *[P("gx", "gy", "gz")] * 2,
        *[P()] * 7,
        *[P("gx", "gy", "gz")] * 2,
        *[P(None, ALL)] * 2,
        P(ALL),
        P(),
    )
    out_specs = (P(None, "gx", "gy", "gz"), P(None, "gx", "gy", "gz"), P(None, ALL))
    return jax.shard_map(shards, mesh=mesh, in_specs=in_specs, out_specs=out_specs, check_vma=False)
```
